128 devices in a mesh: prompt: 8 (over z_hi, y), group: 16 (over x, z_lo, core).
Axes of the slice: x: 4, y: 4, z: 4 (z_hi: 2, z_lo: 2; z = z_hi * 2 + z_lo), core: 2. Of those that a mesh axis runs over, the one named last changes fastest.
Arguments:
- prompt_q: bfloat16 [2048, 1024], P(('prompt', 'group')), may hold values from -6 to 6
- prompt_k: bfloat16 [2048, 1024], P(('prompt', 'group')), may hold values from -6 to 6
- prompt_v: bfloat16 [2048, 1024], P(('prompt', 'group')), may hold values from -6 to 6
- prompt_grad: bfloat16 [2048, 1024], P(('prompt', 'group')), may hold values from -6 to 6
- cont_q: bfloat16 [16, 2048, 1024], P('group', None, 'prompt'), may hold values from -6 to 6
- cont_k: bfloat16 [16, 2048, 1024], P('group', None, 'prompt'), may hold values from -6 to 6
- cont_v: bfloat16 [16, 2048, 1024], P('group', None, 'prompt'), may hold values from -6 to 6
- cont_grad: bfloat16 [16, 2048, 1024], P('group', None, 'prompt'), may hold values from -6 to 6
- lengths: int32 [16], P('group'), may hold values from 256 to 2048, as said below
Outputs:
- prompt_dq: bfloat16 [2048, 1024], P(('prompt', 'group'))
- prompt_dk: bfloat16 [2048, 1024], P(('prompt', 'group'))
- prompt_dv: bfloat16 [2048, 1024], P(('prompt', 'group'))
- cont_dq: bfloat16 [16, 2048, 1024], P('group', None, 'prompt')
- cont_dk: bfloat16 [16, 2048, 1024], P('group', None, 'prompt')
- cont_dv: bfloat16 [16, 2048, 1024], P('group', None, 'prompt')
The draws below stay inside these ranges and needn't reach their ends.
Inputs may be any that keep to these rules, and one draw needn't show every extreme that they name: `lengths`: one member's continuation fills all 2048 rows.
All inputs are finite; a program needn't handle non-finite values.
Results may differ from the reference program's by a relative error of at most 0.024.
Values may be sent and summed in bfloat16 or wider, within the bound.
A program may use at most 64 MiB of HBM per device.

```python
import jax
import jax.numpy as jnp
from jax import lax

HEADS = 8
HEAD_SIZE = 128
PSLICE = 16
CONT = 2048
PROMPT = 2048
MEMBERS = 16


def draw_prompt_k(key, part):
    key = jax.random.fold_in(key, 11)
    sample = jax.random.truncated_normal(key, -6.0, 6.0, (PROMPT, HEADS * HEAD_SIZE), jnp.float32)
    return sample.astype(jnp.bfloat16)


def draw_prompt_q(key, part):
    key = jax.random.fold_in(key, 12)
    sample = jax.random.truncated_normal(key, -6.0, 6.0, (PROMPT, HEADS * HEAD_SIZE), jnp.float32)
    return sample.astype(jnp.bfloat16)


def draw_cont_q(key, part):
    key = jax.random.fold_in(key, 13)
    sample = jax.random.truncated_normal(key, -6.0, 6.0, (MEMBERS, CONT, HEADS * HEAD_SIZE), jnp.float32)
    return sample.astype(jnp.bfloat16)


def draw_lengths(key, part):
    key = jax.random.fold_in(key, 5)
    first_key, second_key = jax.random.split(key)
    lowest = CONT // 8
    drawn = jax.random.randint(first_key, (MEMBERS,), lowest, CONT + 1)
    order = jax.random.permutation(second_key, MEMBERS)
    drawn = drawn.at[order[0]].set(CONT)
    drawn = drawn.at[order[1]].set(lowest)
    return drawn.astype(jnp.int32)


def level_of(own_key, extent, cuts, smallest, largest):
    level, own = 1.0, jax.random.fold_in(own_key, 6)
    for dim, parts in cuts:
        steps = jnp.exp(jax.random.uniform(jax.random.fold_in(own, dim), (parts,), jnp.float32, smallest / len(cuts), largest / len(cuts)))
        level = level * jnp.repeat(steps, extent[dim] // parts).reshape([-1 if axis == dim else 1 for axis in range(len(extent))])
    return level


def centred(own_key, shape, deviation, limit, cuts=(), kind=jnp.bfloat16):
    entries = deviation * jax.random.normal(own_key, shape, jnp.float32)
    if cuts:
        entries = entries * level_of(own_key, shape, cuts, -0.22, 0.18)
    return jnp.clip(entries, -limit, limit).astype(kind)


def setup_inputs(seed: int = 0) -> dict:
    key_list = jax.random.split(jax.random.key(seed), 10)
    return {
        "prompt_q": draw_prompt_q(jax.random.fold_in(key_list[9], 71), 0),
        "prompt_k": draw_prompt_k(jax.random.fold_in(key_list[9], 71), 0),
        "prompt_v": centred(key_list[2], (PROMPT, HEADS * HEAD_SIZE), 1.0, 6.0, ((0, 128),)),
        "prompt_grad": centred(key_list[3], (PROMPT, HEADS * HEAD_SIZE), 1.0, 6.0, ((0, 128),)),
        "cont_q": draw_cont_q(jax.random.fold_in(key_list[9], 71), 0),
        "cont_k": centred(key_list[5], (MEMBERS, CONT, HEADS * HEAD_SIZE), 1.0, 6.0, ((0, 16), (2, 8))),
        "cont_v": centred(key_list[6], (MEMBERS, CONT, HEADS * HEAD_SIZE), 1.0, 6.0, ((0, 16), (2, 8))),
        "cont_grad": centred(key_list[7], (MEMBERS, CONT, HEADS * HEAD_SIZE), 1.0, 6.0, ((0, 16), (2, 8))),
        "lengths": draw_lengths(jax.random.fold_in(key_list[9], 71), 0),
    }


def head_terms(query_rows, grad_rows, key_rows, value_rows, query_pos, key_pos, live_rows):
    scaling = HEAD_SIZE ** -0.5
    scores = jnp.dot(query_rows, key_rows.T, preferred_element_type=jnp.float32) * scaling
    scores = jnp.where(key_pos[None, :] <= query_pos[:, None], scores, -jnp.inf)
    row_max = jnp.max(scores, axis=1, keepdims=True)
    shifted = jnp.exp(scores - row_max)
    attn_probs = shifted / jnp.sum(shifted, axis=1, keepdims=True)
    probs_low = attn_probs.astype(jnp.bfloat16)
    output = jnp.dot(probs_low, value_rows, preferred_element_type=jnp.float32)
    row_delta = jnp.sum(grad_rows.astype(jnp.float32) * output, axis=1, keepdims=True)
    dprob = jnp.dot(grad_rows, value_rows.T, preferred_element_type=jnp.float32)
    dscore = jnp.where(live_rows[:, None], attn_probs * (dprob - row_delta), 0.0)
    dscore_low = dscore.astype(jnp.bfloat16)
    live_probs = jnp.where(live_rows[:, None], probs_low, jnp.zeros_like(probs_low))
    grad_query = jnp.dot(dscore_low, key_rows, preferred_element_type=jnp.float32) * scaling
    grad_key = jnp.dot(dscore_low.T, query_rows, preferred_element_type=jnp.float32) * scaling
    grad_value = jnp.dot(live_probs.T, grad_rows, preferred_element_type=jnp.float32)
    return grad_query, grad_key, grad_value, dscore_low, live_probs


def reference(prompt_q, prompt_k, prompt_v, prompt_grad, cont_q, cont_k, cont_v, cont_grad, lengths):
    scaling = HEAD_SIZE ** -0.5

    def prompt_heads(array):
        return array.reshape(PROMPT, HEADS, HEAD_SIZE).transpose(1, 0, 2)

    def cont_heads(array):
        return array.reshape(MEMBERS, CONT, HEADS, HEAD_SIZE).transpose(2, 0, 1, 3)

    query_p, key_p, value_p, grad_p = prompt_heads(prompt_q), prompt_heads(prompt_k), prompt_heads(prompt_v), prompt_heads(prompt_grad)
    query_c, key_c, value_c, grad_c = cont_heads(cont_q), cont_heads(cont_k), cont_heads(cont_v), cont_heads(cont_grad)
    prompt_pos = jnp.arange(PROMPT, dtype=jnp.int32)
    cont_pos = PROMPT + jnp.arange(CONT, dtype=jnp.int32)
    all_pos = jnp.concatenate([prompt_pos, cont_pos])
    prompt_live = jnp.ones((PROMPT,), dtype=bool)
    stripes = PROMPT // (PSLICE * MEMBERS)

    def per_head(head_index):
        keys_head = key_p[head_index]
        values_head = value_p[head_index]
        self_dq, unused_dk, unused_dv, self_dscore, self_probs = head_terms(
            query_p[head_index], grad_p[head_index], keys_head, values_head, prompt_pos, prompt_pos, prompt_live)
        split_score = self_dscore.astype(jnp.float32).reshape(stripes, MEMBERS, PSLICE, PROMPT)
        split_probs = self_probs.astype(jnp.float32).reshape(stripes, MEMBERS, PSLICE, PROMPT)
        split_query = query_p[head_index].astype(jnp.float32).reshape(stripes, MEMBERS, PSLICE, HEAD_SIZE)
        split_grad = grad_p[head_index].astype(jnp.float32).reshape(stripes, MEMBERS, PSLICE, HEAD_SIZE)
        self_key_parts = jnp.einsum("bgsk,bgsd->gkd", split_score, split_query) * scaling
        self_value_parts = jnp.einsum("bgsk,bgsd->gkd", split_probs, split_grad)

        def per_member(member):
            member_keys = jnp.concatenate([keys_head, key_c[head_index, member]])
            member_values = jnp.concatenate([values_head, value_c[head_index, member]])
            live_rows = jnp.arange(CONT, dtype=jnp.int32) < lengths[member]
            return head_terms(query_c[head_index, member], grad_c[head_index, member], member_keys, member_values, cont_pos, all_pos, live_rows)[:3]

        member_dq, member_dk, member_dv = lax.map(per_member, jnp.arange(MEMBERS, dtype=jnp.int32))
        key_part = lax.optimization_barrier((self_key_parts + member_dk[:, :PROMPT]).astype(jnp.bfloat16))
        value_part = lax.optimization_barrier((self_value_parts + member_dv[:, :PROMPT]).astype(jnp.bfloat16))
        total_dk = jnp.sum(key_part.astype(jnp.float32), axis=0)
        total_dv = jnp.sum(value_part.astype(jnp.float32), axis=0)
        return self_dq, total_dk, total_dv, member_dq, member_dk[:, PROMPT:], member_dv[:, PROMPT:]

    results = lax.map(per_head, jnp.arange(HEADS, dtype=jnp.int32))

    def prompt_out(array):
        return array.transpose(1, 0, 2).reshape(PROMPT, HEADS * HEAD_SIZE).astype(jnp.bfloat16)

    def cont_out(array):
        return array.transpose(1, 2, 0, 3).reshape(MEMBERS, CONT, HEADS * HEAD_SIZE).astype(jnp.bfloat16)

    return (prompt_out(results[0]), prompt_out(results[1]), prompt_out(results[2]),
            cont_out(results[3]), cont_out(results[4]), cont_out(results[5]))
```

```python
import functools
import math

import jax
import jax.numpy as jnp
from jax import lax
from jax.experimental import pallas as pl
from jax.experimental.pallas import tpu as pltpu
from jax.sharding import PartitionSpec as P

F = jnp.float32
B = jnp.bfloat16
HS = 128
NP = 2048
NC = 2048
QB = 256
NB = NC // QB
PQ = 128
NQ = NC + PQ
HEADS = 8
CHIPS = 8
SCALE = HS**-0.5
SCALE2 = SCALE * math.log2(math.e)
NEG = -1e30


def nt(a, b):
    return lax.dot_general(a, b, (((1,), (1,)), ((), ())), preferred_element_type=F)


def nn(a, b):
    return jnp.dot(a, b, preferred_element_type=F)


def fold(x, op):
    return op(x.reshape(x.shape[0] // 8, 8, x.shape[1]), axis=0)


def rowmax(x):
    return jnp.max(x, axis=0, keepdims=True)


def rowsum(x):
    return jnp.sum(x, axis=0, keepdims=True)


def kernel(
    pq, pk, pv, pg, cq, ck, cv, cg, lens,
    o_pdq, o_pdk, o_pdv, o_dq, o_dk, o_dv,
    q_c, k_c, v_c, g_c, kt_c, kt_p, kv, qg, send_kv, send_qg,
    sbuf, e_p, e_c, d_p, d_c, gp, qp, gc, qc, stat, dqt,
    st_sib, r_sib, st_own, r_chip, outs, ret,
    in_sem, s1, r1, s2, r2, s3, r3, s4, r4, s5, r5, s6, r6,
):
    p = lax.axis_index("prompt")
    g = lax.axis_index("group")
    core = lax.rem(g, 2)
    other = 1 - core
    chip = g // 2
    sibling = chip * 2 + other

    def peer_p(d):
        return lax.rem(p + d, HEADS)

    def peer_chip(d):
        return lax.rem(chip + d, CHIPS)

    def back_chip(d):
        return lax.rem(chip + CHIPS - d, CHIPS)

    def remote(src, dst, ssem, rsem, dev):
        return pltpu.make_async_remote_copy(
            src_ref=src, dst_ref=dst, send_sem=ssem, recv_sem=rsem,
            device_id=dev, device_id_type=pl.DeviceIdType.MESH,
        )

    loads = [
        pltpu.make_async_copy(src.at[0], dst, in_sem.at[i])
        for i, (src, dst) in enumerate(((cq, q_c), (ck, k_c), (cv, v_c), (cg, g_c)))
    ]
    for load in loads:
        load.start()

    barrier = pltpu.get_barrier_semaphore()
    for d in range(1, HEADS):
        pl.semaphore_signal(barrier, inc=1, device_id=(peer_p(d), g), device_id_type=pl.DeviceIdType.MESH)
    for d in range(1, CHIPS):
        pl.semaphore_signal(
            barrier, inc=1, device_id=(p, peer_chip(d) * 2 + core), device_id_type=pl.DeviceIdType.MESH
        )
    pl.semaphore_signal(barrier, inc=1, device_id=(p, sibling), device_id_type=pl.DeviceIdType.MESH)

    for h in range(HEADS):
        cols = slice(h * HS, (h + 1) * HS)
        send_kv[h, 0] = pk[:, cols]
        send_kv[h, 1] = pv[:, cols]
        send_qg[h, 0] = pq[:, cols]
        send_qg[h, 1] = pg[:, cols]
    kv[:, core, chip, p] = send_kv[p]
    qg[:, p] = send_qg[p]

    pl.semaphore_wait(barrier, HEADS - 1 + CHIPS)

    c1, c1q = [], []
    for d in range(1, HEADS):
        dev = (peer_p(d), g)
        c1.append(remote(send_kv.at[peer_p(d)], kv.at[:, core, chip, p], s1.at[0, d], r1.at[0, d], dev))
        c1q.append(remote(send_qg.at[peer_p(d)], qg.at[:, p], s1.at[1, d], r1.at[1, d], dev))
    for c in c1:
        c.start()
    for c in c1q:
        c.start()

    length = lens[0]
    for load in loads:
        load.wait()
    kt_c[...] = k_c[...].T

    diagonal = lax.broadcasted_iota(jnp.int32, (QB, QB), 0) <= lax.broadcasted_iota(jnp.int32, (QB, QB), 1)

    def cont_block(i):
        qs = slice(i * QB, (i + 1) * QB)
        q = q_c[qs, :]
        gr = g_c[qs, :]
        mx = jnp.full((8, QB), NEG, F)
        for j in range(i + 1):
            r = slice(j * QB, (j + 1) * QB)
            s = nt(k_c[r, :], q)
            if j == i:
                s = jnp.where(diagonal, s, NEG)
            sbuf[r, :] = s
            mx = jnp.maximum(mx, fold(s, jnp.max))
        m = rowmax(mx) * SCALE2
        l = jnp.zeros((8, QB), F)
        w = jnp.zeros((8, QB), F)
        for j in range(i + 1):
            r = slice(j * QB, (j + 1) * QB)
            e = jnp.exp2(sbuf[r, :] * SCALE2 - m)
            e_c[r, qs] = e.astype(B)
            dp = nt(v_c[r, :], gr).astype(B)
            d_c[r, qs] = dp
            l = l + fold(e, jnp.sum)
            w = w + fold(e * dp.astype(F), jnp.sum)
        stat[i, 0:1, :] = m
        stat[i, 1:2, :] = rowsum(l)
        stat[i, 2:3, :] = rowsum(w)

    for i in range(5):
        cont_block(i)

    for c in c1:
        c.wait()

    def block(which_core, which_chip):
        return kv.at[:, which_core, which_chip]

    c2 = [
        remote(block(core, chip), block(core, chip), s2.at[d], r2.at[d], (p, peer_chip(d) * 2 + core))
        for d in range(1, CHIPS)
    ]
    for c in c2:
        c.start()
    c3 = [remote(block(core, chip), block(core, chip), s3.at[0], r3.at[0], (p, sibling))]
    c3[0].start()

    for i in range(5, NB):
        cont_block(i)

    for d in range(1, CHIPS):
        c2[d - 1].wait_recv()
        at = block(core, back_chip(d))
        c = remote(at, at, s3.at[d], r3.at[d], (p, sibling))
        c.start()
        c3.append(c)
    for c in c1q:
        c.wait()
    for c in c3:
        c.wait_recv()

    def kv_rows(which, c):
        return kv[which, c // 4, (c % 4) * 2 : (c % 4) * 2 + 2].reshape(QB, HS)

    for c in range(NP // QB):
        kt_p[:, c * QB : (c + 1) * QB] = kv_rows(0, c).T

    def prompt_part(qs, qn, q, gr, mask, m_c, l_c, w_c):
        mx = jnp.full((8, qn), NEG, F)
        for c in range(NP // QB):
            s = nt(kv_rows(0, c), q)
            if mask is not None:
                s = jnp.where(mask(c), s, NEG)
            sbuf[c * QB : (c + 1) * QB, 0:qn] = s
            mx = jnp.maximum(mx, fold(s, jnp.max))
        m = rowmax(mx) * SCALE2
        if m_c is not None:
            m = jnp.maximum(m, m_c)
        l = jnp.zeros((8, qn), F)
        w = jnp.zeros((8, qn), F)
        for c in range(NP // QB):
            r = slice(c * QB, (c + 1) * QB)
            e = jnp.exp2(sbuf[r, 0:qn] * SCALE2 - m)
            e_p[r, qs] = e.astype(B)
            dp = nt(kv_rows(1, c), gr)
            sbuf[r, 0:qn] = dp
            l = l + fold(e, jnp.sum)
            w = w + fold(e * dp, jnp.sum)
        l = rowsum(l)
        w = rowsum(w)
        alpha = None
        if m_c is not None:
            alpha = jnp.exp2(m_c - m)
            l = l + alpha * l_c
            w = w + alpha * w_c
        inv = 1.0 / l
        delta = w * inv
        acc = jnp.zeros((HS, qn), F)
        for c in range(NP // QB):
            r = slice(c * QB, (c + 1) * QB)
            ds = e_p[r, qs] * (sbuf[r, 0:qn] - delta).astype(B)
            d_p[r, qs] = ds
            acc = acc + nn(kt_p[:, r], ds)
        return acc, inv, delta, alpha

    def column(row, qn):
        return jnp.broadcast_to(row, (HS, qn)).T

    q0 = qg[0].reshape(PQ, HS)
    g0 = qg[1].reshape(PQ, HS)

    def prompt_mask(c):
        row = lax.broadcasted_iota(jnp.int32, (QB, 1), 0)
        key_group = ((c % 4) * 2 + row // HS) * 2 + c // 4
        key_pos = ((row % HS) // 16) * 256 + key_group * 16 + row % 16
        col = lax.broadcasted_iota(jnp.int32, (1, PQ), 1)
        query_pos = (col // 16) * 256 + g * 16 + col % 16
        return key_pos <= query_pos

    acc, inv, _, _ = prompt_part(slice(NC, NQ), PQ, q0, g0, prompt_mask, None, None, None)
    outs[0] = (acc * (inv * SCALE)).T.astype(B).reshape(HEADS, 16, HS)
    inv_col = column(inv, PQ)
    gp[NC:NQ, :] = (g0.astype(F) * inv_col).astype(B)
    qp[NC:NQ, :] = (q0.astype(F) * (inv_col * SCALE)).astype(B)

    def member_block(i, carry):
        off = pl.multiple_of(i * QB, QB)
        qs = pl.ds(off, QB)
        q = q_c[qs, :]
        gr = g_c[qs, :]
        row = stat[i]
        acc, inv, delta, alpha = prompt_part(qs, QB, q, gr, None, row[0:1], row[1:2], row[2:3])
        live = (lax.broadcasted_iota(jnp.int32, (1, QB), 1) + off) < length
        inv = jnp.where(live, inv, 0.0)
        inv_c = inv * alpha
        stat[i, 3:4, :] = delta
        stat[i, 4:5, :] = inv_c
        dqt[i] = acc * inv
        inv_col = column(inv, QB)
        inv_c_col = column(inv_c, QB)
        qf = q.astype(F) * SCALE
        gf = gr.astype(F)
        gp[qs, :] = (gf * inv_col).astype(B)
        qp[qs, :] = (qf * inv_col).astype(B)
        gc[qs, :] = (gf * inv_c_col).astype(B)
        qc[qs, :] = (qf * inv_c_col).astype(B)
        return carry

    lax.fori_loop(0, NB, member_block, 0)

    half = NP // 4

    def parts(which_core, u):
        r = pl.ds(pl.multiple_of(which_core * (NP // 2) + u * half, half), half)
        return nn(d_p[r, :], qp[...]), nn(e_p[r, :], gp[...])

    c4 = []
    for u in range(2):
        dk, dv = parts(other, u)
        st_sib[u, 0] = dk.astype(B)
        st_sib[u, 1] = dv.astype(B)
        c = remote(st_sib.at[u], r_sib.at[u], s4.at[u], r4.at[u], (p, sibling))
        c.start()
        c4.append(c)
    for u in range(2):
        dk, dv = parts(core, u)
        c4[u].wait_recv()
        st_own[u, 0] = (dk + r_sib[u, 0].astype(F)).astype(B).reshape(4, HS, HS)
        st_own[u, 1] = (dv + r_sib[u, 1].astype(F)).astype(B).reshape(4, HS, HS)
        for k in range(4):
            to = u * 4 + k
            d = lax.rem(to + CHIPS - chip, CHIPS)

            @pl.when(d == 0)
            def _():
                r_chip[0] = st_own[u, :, k]

            @pl.when(d != 0)
            def _():
                remote(
                    st_own.at[u, :, k], r_chip.at[d], s5.at[d], r5.at[d], (p, to * 2 + core)
                ).start()

    def cont_grads(i):
        qs = slice(i * QB, (i + 1) * QB)
        delta = stat[i, 3:4, :]
        inv_c = stat[i, 4:5, :]
        acc = jnp.zeros((HS, QB), F)
        for j in range(i + 1):
            r = slice(j * QB, (j + 1) * QB)
            ds = e_c[r, qs] * (d_c[r, qs].astype(F) - delta).astype(B)
            d_c[r, qs] = ds
            acc = acc + nn(kt_c[:, r], ds)
        o_dq[0, qs, :] = ((dqt[i] + acc * inv_c) * SCALE).T.astype(B)

    for i in range(NB):
        cont_grads(i)

    def cont_key(j):
        r = slice(j * QB, (j + 1) * QB)
        qs = slice(j * QB, NC)
        o_dk[0, r, :] = nn(d_c[r, qs], qc[qs, :]).astype(B)
        o_dv[0, r, :] = nn(e_c[r, qs], gc[qs, :]).astype(B)

    for j in range(0, 3):
        cont_key(j)

    for d in range(1, CHIPS):
        remote(r_chip.at[d], r_chip.at[d], s5.at[d], r5.at[d], (p, sibling)).wait_recv()
    total = r_chip[0].astype(F)
    for d in range(1, CHIPS):
        total = total + r_chip[d].astype(F)
    outs[1:3] = total.astype(B).reshape(2, HEADS, 16, HS)

    c6 = []
    for d in range(1, HEADS):
        c = remote(outs.at[:, peer_p(d)], ret.at[:, p], s6.at[d], r6.at[d], (peer_p(d), g))
        c.start()
        c6.append(c)
    ret[:, p] = outs[:, p]

    for j in range(3, NB):
        cont_key(j)

    for c in c6:
        c.wait_recv()
    for h in range(HEADS):
        cols = slice(h * HS, (h + 1) * HS)
        o_pdq[:, cols] = ret[0, h]
        o_pdk[:, cols] = ret[1, h]
        o_pdv[:, cols] = ret[2, h]

    for c in c2:
        c.wait_send()
    for c in c3:
        c.wait_send()
    for c in c4:
        c.wait_send()
    for d in range(1, CHIPS):
        remote(r_chip.at[d], r_chip.at[d], s5.at[d], r5.at[d], (p, sibling)).wait_send()
    for c in c6:
        c.wait_send()


def shards(prompt_q, prompt_k, prompt_v, prompt_grad, cont_q, cont_k, cont_v, cont_grad, lengths):
    vm = pl.BlockSpec(memory_space=pltpu.VMEM)
    anym = pl.BlockSpec(memory_space=pl.ANY)
    sm = pl.BlockSpec(memory_space=pltpu.SMEM)
    small = jax.ShapeDtypeStruct((16, HEADS * HS), B)
    large = jax.ShapeDtypeStruct((1, NC, HS), B)
    dma = pltpu.SemaphoreType.DMA
    vmem = pltpu.VMEM
    return pl.pallas_call(
        kernel,
        out_shape=[small] * 3 + [large] * 3,
        in_specs=[vm] * 4 + [anym] * 4 + [sm],
        out_specs=[vm] * 6,
        scratch_shapes=[vmem((NC, HS), B)] * 4
        + [
            vmem((HS, NC), B),
            vmem((HS, NP), B),
            vmem((2, 2, CHIPS, HEADS, 16, HS), B),
            vmem((2, HEADS, 16, HS), B),
            vmem((HEADS, 2, 16, HS), B),
            vmem((HEADS, 2, 16, HS), B),
            vmem((NP, QB), F),
            vmem((NP, NQ), B),
            vmem((NC, NC), B),
            vmem((NP, NQ), B),
            vmem((NC, NC), B),
            vmem((NQ, HS), B),
            vmem((NQ, HS), B),
            vmem((NC, HS), B),
            vmem((NC, HS), B),
            vmem((NB, 8, QB), F),
            vmem((NB, HS, QB), F),
            vmem((2, 2, NP // 4, HS), B),
            vmem((2, 2, NP // 4, HS), B),
            vmem((2, 2, 4, HS, HS), B),
            vmem((CHIPS, 2, HS, HS), B),
            vmem((3, HEADS, 16, HS), B),
            vmem((3, HEADS, 16, HS), B),
            dma((4,)),
            dma((2, HEADS)),
            dma((2, HEADS)),
        ]
        + [dma((CHIPS,))] * 4
        + [dma((2,))] * 2
        + [dma((CHIPS,))] * 2
        + [dma((HEADS,))] * 2,
        compiler_params=pltpu.CompilerParams(
            collective_id=0, has_side_effects=True, vmem_limit_bytes=60 * 2**20
        ),
    )(prompt_q, prompt_k, prompt_v, prompt_grad, cont_q, cont_k, cont_v, cont_grad, lengths)


def solution(mesh):
    rows = P(("prompt", "group"), None)
    member = P("group", None, "prompt")
    return jax.shard_map(
        shards,
        mesh=mesh,
        in_specs=(rows,) * 4 + (member,) * 4 + (P("group"),),
        out_specs=(rows,) * 3 + (member,) * 3,
        check_vma=False,
    )
```

```python
import functools
import math

import jax
import jax.numpy as jnp
from jax import lax
from jax.experimental import pallas as pl
from jax.experimental.pallas import tpu as pltpu
from jax.sharding import PartitionSpec as P

F = jnp.float32
B = jnp.bfloat16
HS = 128
NP = 2048
NC = 2048
QB = 256
NB = NC // QB
PQ = 128
NQ = NC + PQ
HEADS = 8
CHIPS = 8
MESH = pl.DeviceIdType.MESH
SCALE = HS**-0.5
SCALE2 = SCALE * math.log2(math.e)
NEG = -1e30


def nt(a, b):
    return lax.dot_general(a, b, (((1,), (1,)), ((), ())), preferred_element_type=F)


def nn(a, b):
    return jnp.dot(a, b, preferred_element_type=F)


def fold(x, op):
    return op(x.reshape(x.shape[0] // 8, 8, x.shape[1]), axis=0)


def rowmax(x):
    return jnp.max(x, axis=0, keepdims=True)


def rowsum(x):
    return jnp.sum(x, axis=0, keepdims=True)


def kernel(
    pq, pk, pv, pg, cq, ck, cv, cg, lens,
    o_pdq, o_pdk, o_pdv, o_dq, o_dk, o_dv,
    q_c, k_c, v_c, g_c, rows_in, kt_c, kt_p, kv, qg, send_kv, send_qg,
    sbuf, e_p, e_c, d_p, d_c, gp, qp, gc, qc, stat, dqt,
    st_sib, r_sib, st_own, r_own, dq_out, dq_in,
    lens_in, in_sem, s1, r1, s2, r2, s3, r3, s4, r4, s5, r5, s6, r6,
):
    p = lax.axis_index("prompt")
    g = lax.axis_index("group")
    core = lax.rem(g, 2)
    other = 1 - core
    chip = g // 2
    sibling = chip * 2 + other

    def peer_p(d):
        return lax.rem(p + d, HEADS)

    def peer_chip(d):
        return lax.rem(chip + d, CHIPS)

    def back_chip(d):
        return lax.rem(chip + CHIPS - d, CHIPS)

    def remote(src, dst, ssem, rsem, dev):
        return pltpu.make_async_remote_copy(
            src_ref=src, dst_ref=dst, send_sem=ssem, recv_sem=rsem, device_id=dev, device_id_type=MESH
        )

    barrier = pltpu.get_barrier_semaphore()
    for dc in range(CHIPS):
        for dp in range(HEADS):
            if dc or dp:
                pl.semaphore_signal(
                    barrier, inc=1, device_id=(peer_p(dp), peer_chip(dc) * 2 + core), device_id_type=MESH
                )
    pl.semaphore_signal(barrier, inc=1, device_id=(p, sibling), device_id_type=MESH)

    loads = [
        pltpu.make_async_copy(src, dst, in_sem.at[i])
        for i, (src, dst) in enumerate(
            (
                (ck.at[0], k_c), (cq.at[0], q_c), (cv.at[0], v_c), (cg.at[0], g_c),
                (pk, rows_in.at[0]), (pv, rows_in.at[1]), (pq, rows_in.at[2]), (pg, rows_in.at[3]),
                (lens, lens_in),
            )
        )
    ]
    for load in loads:
        load.start()
    for load in loads:
        load.wait()
    length = lens_in[0]

    for h in range(HEADS):
        cols = slice(h * HS, (h + 1) * HS)
        send_kv[h, 0] = rows_in[0, :, cols]
        send_kv[h, 1] = rows_in[1, :, cols]
        send_qg[h, 0] = rows_in[2, :, cols]
        send_qg[h, 1] = rows_in[3, :, cols]
    kv[0, chip, p] = send_kv[p]
    qg[p] = send_qg[p]

    diagonal = lax.broadcasted_iota(jnp.int32, (QB, QB), 0) <= lax.broadcasted_iota(jnp.int32, (QB, QB), 1)

    def cont_block(i):
        qs = slice(i * QB, (i + 1) * QB)
        q = q_c[qs, :]
        gr = g_c[qs, :]
        mx = jnp.full((8, QB), NEG, F)
        for j in range(i + 1):
            r = slice(j * QB, (j + 1) * QB)
            s = nt(k_c[r, :], q)
            if j == i:
                s = jnp.where(diagonal, s, NEG)
            sbuf[r, :] = s
            mx = jnp.maximum(mx, fold(s, jnp.max))
        m = rowmax(mx) * SCALE2
        l = jnp.zeros((8, QB), F)
        w = jnp.zeros((8, QB), F)
        for j in range(i + 1):
            r = slice(j * QB, (j + 1) * QB)
            e = jnp.exp2(sbuf[r, :] * SCALE2 - m)
            e_c[r, qs] = e.astype(B)
            dp = nt(v_c[r, :], gr).astype(B)
            d_c[r, qs] = dp
            l = l + fold(e, jnp.sum)
            w = w + fold(e * dp.astype(F), jnp.sum)
        stat[i, 0:1, :] = m
        stat[i, 1:2, :] = rowsum(l)
        stat[i, 2:3, :] = rowsum(w)

    for i in range(NB):
        cont_block(i)

    pl.semaphore_wait(barrier, HEADS * CHIPS)

    for dc in range(CHIPS):
        for dp in range(HEADS):
            if dc or dp:
                remote(
                    send_kv.at[peer_p(dp)], kv.at[0, chip, p], s1.at[dc], r1.at[dc],
                    (peer_p(dp), peer_chip(dc) * 2 + core),
                ).start()
        if dc == 0:
            for dp in range(1, HEADS):
                remote(send_qg.at[peer_p(dp)], qg.at[p], s2.at[0], r2.at[0], (peer_p(dp), g)).start()

    kt_c[...] = k_c[...].T

    forwards = []
    for dc in range(CHIPS):
        at = kv.at[0, back_chip(dc)]
        whole = at if dc else kv.at[0, back_chip(dc), 0 : HEADS - 1]
        remote(whole, whole, s1.at[dc], r1.at[dc], (p, sibling)).wait()
        c = remote(at, kv.at[1, back_chip(dc)], s3.at[dc], r3.at[dc], (p, sibling))
        c.start()
        forwards.append(c)
    seven = qg.at[0 : HEADS - 1]
    remote(seven, seven, s2.at[0], r2.at[0], (p, sibling)).wait()

    def kv_rows(which, c):
        return kv[c // 4, (c % 4) * 2 : (c % 4) * 2 + 2, :, which].reshape(QB, HS)

    for c in range(NP // QB):
        if c == 4:
            for f in forwards:
                f.wait_recv()
        kt_p[:, c * QB : (c + 1) * QB] = kv_rows(0, c).T

    def prompt_part(qs, qn, q, gr, mask, m_c, l_c, w_c):
        mx = jnp.full((8, qn), NEG, F)
        for c in range(NP // QB):
            s = nt(kv_rows(0, c), q)
            if mask is not None:
                s = jnp.where(mask(c), s, NEG)
            sbuf[c * QB : (c + 1) * QB, 0:qn] = s
            mx = jnp.maximum(mx, fold(s, jnp.max))
        m = rowmax(mx) * SCALE2
        if m_c is not None:
            m = jnp.maximum(m, m_c)
        l = jnp.zeros((8, qn), F)
        w = jnp.zeros((8, qn), F)
        for c in range(NP // QB):
            r = slice(c * QB, (c + 1) * QB)
            e = jnp.exp2(sbuf[r, 0:qn] * SCALE2 - m)
            e_p[r, qs] = e.astype(B)
            dp = nt(kv_rows(1, c), gr)
            sbuf[r, 0:qn] = dp
            l = l + fold(e, jnp.sum)
            w = w + fold(e * dp, jnp.sum)
        l = rowsum(l)
        w = rowsum(w)
        alpha = None
        if m_c is not None:
            alpha = jnp.exp2(m_c - m)
            l = l + alpha * l_c
            w = w + alpha * w_c
        inv = 1.0 / l
        delta = w * inv
        acc = jnp.zeros((HS, qn), F)
        for c in range(NP // QB):
            r = slice(c * QB, (c + 1) * QB)
            ds = e_p[r, qs] * (sbuf[r, 0:qn] - delta).astype(B)
            d_p[r, qs] = ds
            acc = acc + nn(kt_p[:, r], ds)
        return acc, inv, delta, alpha

    def column(row, qn):
        return jnp.broadcast_to(row, (HS, qn)).T

    q0 = qg[:, 0].reshape(PQ, HS)
    g0 = qg[:, 1].reshape(PQ, HS)

    def prompt_mask(c):
        row = lax.broadcasted_iota(jnp.int32, (QB, 1), 0)
        key_core = core if c < 4 else other
        key_group = ((c % 4) * 2 + row // HS) * 2 + key_core
        key_pos = ((row % HS) // 16) * 256 + key_group * 16 + row % 16
        col = lax.broadcasted_iota(jnp.int32, (1, PQ), 1)
        query_pos = (col // 16) * 256 + g * 16 + col % 16
        return key_pos <= query_pos

    acc, inv, _, _ = prompt_part(slice(NC, NQ), PQ, q0, g0, prompt_mask, None, None, None)
    dq_out[...] = (acc * (inv * SCALE)).T.astype(B).reshape(HEADS, 16, HS)
    for dp in range(1, HEADS):
        remote(dq_out.at[peer_p(dp)], dq_in.at[p], s6.at[0], r6.at[0], (peer_p(dp), g)).start()
    dq_in[p] = dq_out[p]
    inv_col = column(inv, PQ)
    gp[NC:NQ, :] = (g0.astype(F) * inv_col).astype(B)
    qp[NC:NQ, :] = (q0.astype(F) * (inv_col * SCALE)).astype(B)

    def member_block(i, carry):
        off = pl.multiple_of(i * QB, QB)
        qs = pl.ds(off, QB)
        q = q_c[qs, :]
        gr = g_c[qs, :]
        row = stat[i]
        acc, inv, delta, alpha = prompt_part(qs, QB, q, gr, None, row[0:1], row[1:2], row[2:3])
        live = (lax.broadcasted_iota(jnp.int32, (1, QB), 1) + off) < length
        inv = jnp.where(live, inv, 0.0)
        inv_c = inv * alpha
        stat[i, 3:4, :] = delta
        stat[i, 4:5, :] = inv_c
        dqt[i] = acc * inv
        inv_col = column(inv, QB)
        inv_c_col = column(inv_c, QB)
        qf = q.astype(F) * SCALE
        gf = gr.astype(F)
        gp[qs, :] = (gf * inv_col).astype(B)
        qp[qs, :] = (qf * inv_col).astype(B)
        gc[qs, :] = (gf * inv_c_col).astype(B)
        qc[qs, :] = (qf * inv_c_col).astype(B)
        return carry

    lax.fori_loop(0, NB, member_block, 0)

    half = NP // 4

    def parts(which, u):
        r = slice(which * (NP // 2) + u * half, which * (NP // 2) + (u + 1) * half)
        return nn(d_p[r, :], qp[...]), nn(e_p[r, :], gp[...])

    to_sibling = []
    for u in range(2):
        dk, dv = parts(1, u)
        st_sib[u, 0] = dk.astype(B)
        st_sib[u, 1] = dv.astype(B)
        c = remote(st_sib.at[u], r_sib.at[u], s4.at[u], r4.at[u], (p, sibling))
        c.start()
        to_sibling.append(c)
    slot = p * CHIPS + chip
    for u in range(2):
        dk, dv = parts(0, u)
        to_sibling[u].wait_recv()
        st_own[u * 4 : u * 4 + 4, :, 0] = (dk + r_sib[u, 0].astype(F)).astype(B).reshape(4, HEADS, 16, HS)
        st_own[u * 4 : u * 4 + 4, :, 1] = (dv + r_sib[u, 1].astype(F)).astype(B).reshape(4, HEADS, 16, HS)
        for k in range(4):
            to = u * 4 + k
            for dp in range(1, HEADS):
                remote(
                    st_own.at[to, peer_p(dp)], r_own.at[slot], s5.at[0], r5.at[0],
                    (peer_p(dp), to * 2 + core),
                ).start()

            @pl.when(chip != to)
            def _():
                remote(
                    st_own.at[to, p], r_own.at[slot], s5.at[0], r5.at[0], (p, to * 2 + core)
                ).start()

    r_own[slot] = st_own[chip, p]

    def cont_grads(i):
        qs = slice(i * QB, (i + 1) * QB)
        delta = stat[i, 3:4, :]
        inv_c = stat[i, 4:5, :]
        acc = jnp.zeros((HS, QB), F)
        for j in range(i + 1):
            r = slice(j * QB, (j + 1) * QB)
            ds = e_c[r, qs] * (d_c[r, qs].astype(F) - delta).astype(B)
            d_c[r, qs] = ds
            acc = acc + nn(kt_c[:, r], ds)
        o_dq[0, qs, :] = ((dqt[i] + acc * inv_c) * SCALE).T.astype(B)

    for i in range(NB):
        cont_grads(i)

    def cont_key(j):
        r = slice(j * QB, (j + 1) * QB)
        qs = slice(j * QB, NC)
        o_dk[0, r, :] = nn(d_c[r, qs], qc[qs, :]).astype(B)
        o_dv[0, r, :] = nn(e_c[r, qs], gc[qs, :]).astype(B)

    for j in range(NB):
        cont_key(j)

    seven = dq_in.at[0 : HEADS - 1]
    remote(seven, seven, s6.at[0], r6.at[0], (p, sibling)).wait()
    for h in range(HEADS):
        o_pdq[:, h * HS : (h + 1) * HS] = dq_in[h]

    arrived = r_own.at[0 : HEADS * CHIPS - 1]
    remote(arrived, arrived, s5.at[0], r5.at[0], (p, sibling)).wait()
    for h in range(HEADS):
        cols = slice(h * HS, (h + 1) * HS)
        total = jnp.sum(r_own[h * CHIPS : (h + 1) * CHIPS].astype(F), axis=0)
        o_pdk[:, cols] = total[0].astype(B)
        o_pdv[:, cols] = total[1].astype(B)

    for c in forwards:
        c.wait_send()
    for c in to_sibling:
        c.wait_send()


def hand_over(*refs):
    ins, outs, sem = refs[:6], refs[6:12], refs[12]
    copies = [pltpu.make_async_copy(a, b, sem.at[i]) for i, (a, b) in enumerate(zip(ins, outs))]
    for c in copies:
        c.start()
    for c in copies:
        c.wait()


def shards(prompt_q, prompt_k, prompt_v, prompt_grad, cont_q, cont_k, cont_v, cont_grad, lengths):
    vm = pl.BlockSpec(memory_space=pltpu.VMEM)
    hbm = pl.BlockSpec(memory_space=pltpu.HBM)
    dma = pltpu.SemaphoreType.DMA
    vmem = pltpu.VMEM
    shapes = [(16, HEADS * HS)] * 3 + [(1, NC, HS)] * 3
    results = pl.pallas_call(
        kernel,
        out_shape=[vmem(shape, B) for shape in shapes],
        in_specs=[hbm] * 9,
        out_specs=[vm] * 6,
        scratch_shapes=[vmem((NC, HS), B)] * 4
        + [
            vmem((4, 16, HEADS * HS), B),
            vmem((HS, NC), B),
            vmem((HS, NP), B),
            vmem((2, CHIPS, HEADS, 2, 16, HS), B),
            vmem((HEADS, 2, 16, HS), B),
            vmem((HEADS, 2, 16, HS), B),
            vmem((HEADS, 2, 16, HS), B),
            vmem((NP, QB), F),
            vmem((NP, NQ), B),
            vmem((NC, NC), B),
            vmem((NP, NQ), B),
            vmem((NC, NC), B),
            vmem((NQ, HS), B),
            vmem((NQ, HS), B),
            vmem((NC, HS), B),
            vmem((NC, HS), B),
            vmem((NB, 8, QB), F),
            vmem((NB, HS, QB), F),
            vmem((2, 2, NP // 4, HS), B),
            vmem((2, 2, NP // 4, HS), B),
            vmem((CHIPS, HEADS, 2, 16, HS), B),
            vmem((HEADS * CHIPS, 2, 16, HS), B),
            vmem((HEADS, 16, HS), B),
            vmem((HEADS, 16, HS), B),
            pltpu.SMEM((1,), jnp.int32),
            dma((9,)),
            dma((CHIPS,)),
            dma((CHIPS,)),
            dma((1,)),
            dma((1,)),
            dma((CHIPS,)),
            dma((CHIPS,)),
            dma((2,)),
            dma((2,)),
        ]
        + [dma((1,))] * 4,
        compiler_params=pltpu.CompilerParams(
            collective_id=0, has_side_effects=True, vmem_limit_bytes=54 * 2**20
        ),
    )(prompt_q, prompt_k, prompt_v, prompt_grad, cont_q, cont_k, cont_v, cont_grad, lengths)
    return pl.pallas_call(
        hand_over,
        out_shape=[jax.ShapeDtypeStruct(shape, B) for shape in shapes],
        in_specs=[vm] * 6,
        out_specs=[hbm] * 6,
        scratch_shapes=[dma((6,))],
    )(*[pltpu.with_memory_space_constraint(x, pltpu.VMEM) for x in results])


def solution(mesh):
    rows = P(("prompt", "group"), None)
    member = P("group", None, "prompt")
    return jax.shard_map(
        shards,
        mesh=mesh,
        in_specs=(rows,) * 4 + (member,) * 4 + (P("group"),),
        out_specs=(rows,) * 3 + (member,) * 3,
        check_vma=False,
    )
```

```python
import functools
import math

import jax
import jax.numpy as jnp
from jax import lax
from jax.experimental import pallas as pl
from jax.experimental.pallas import tpu as pltpu
from jax.sharding import PartitionSpec as P

F = jnp.float32
B = jnp.bfloat16
HS = 128
NP = 2048
NC = 2048
CB = 256
QB = 512
WB = 1024
GK = NP // 2
PQ = 128
NQ = NC + PQ
HEADS = 8
CHIPS = 8
MESH = pl.DeviceIdType.MESH
SCALE = HS**-0.5
SCALE2 = SCALE * math.log2(math.e)
NEG = -1e30


def nt(a, b):
    return lax.dot_general(a, b, (((1,), (1,)), ((), ())), preferred_element_type=F)


def nn(a, b):
    return jnp.dot(a, b, preferred_element_type=F)


def fold(x, op):
    return op(x.reshape(x.shape[0] // 8, 8, x.shape[1]), axis=0)


def rowmax(x):
    return jnp.max(x, axis=0, keepdims=True)


def rowsum(x):
    return jnp.sum(x, axis=0, keepdims=True)


def kernel(
    pq, pk, pv, pg, cq, ck, cv, cg, lens,
    o_pdq, o_pdk, o_pdv, o_dq, o_dk, o_dv,
    q_all, k_c, v_c, g_all, rows_in, kt_c, kt_p, kv, qg, send_kv, send_qg,
    sbuf, e_p, e_c, d_p, d_c, stat,
    st_sib, r_sib, st_own, r_own, dq_out, dq_in,
    lens_in, in_sem, s1, r1, s2, r2, s3, r3, s4, r4, s5, r5, s6, r6,
):
    p = lax.axis_index("prompt")
    g = lax.axis_index("group")
    core = lax.rem(g, 2)
    other = 1 - core
    chip = g // 2
    sibling = chip * 2 + other

    def peer_p(d):
        return lax.rem(p + d, HEADS)

    def peer_chip(d):
        return lax.rem(chip + d, CHIPS)

    def back_chip(d):
        return lax.rem(chip + CHIPS - d, CHIPS)

    def remote(src, dst, ssem, rsem, dev):
        return pltpu.make_async_remote_copy(
            src_ref=src, dst_ref=dst, send_sem=ssem, recv_sem=rsem, device_id=dev, device_id_type=MESH
        )

    loads = [
        pltpu.make_async_copy(src, dst, in_sem.at[i])
        for i, (src, dst) in enumerate(
            (
                (pk, rows_in.at[0]), (pv, rows_in.at[1]), (pq, rows_in.at[2]), (pg, rows_in.at[3]),
                (ck.at[0], k_c), (cq.at[0], q_all.at[0:NC]), (cv.at[0], v_c), (cg.at[0], g_all.at[0:NC]),
                (lens, lens_in),
            )
        )
    ]
    for load in loads:
        load.start()

    barrier = pltpu.get_barrier_semaphore()
    for dc in range(CHIPS):
        for dp in range(HEADS):
            if dc or dp:
                pl.semaphore_signal(
                    barrier, inc=1, device_id=(peer_p(dp), peer_chip(dc) * 2 + core), device_id_type=MESH
                )
    pl.semaphore_signal(barrier, inc=1, device_id=(p, sibling), device_id_type=MESH)

    for load in loads[:4]:
        load.wait()
    for h in range(HEADS):
        cols = slice(h * HS, (h + 1) * HS)
        send_kv[h, 0] = rows_in[0, :, cols]
        send_kv[h, 1] = rows_in[1, :, cols]
        send_qg[h, 0] = rows_in[2, :, cols]
        send_qg[h, 1] = rows_in[3, :, cols]
    kv[0, 0, p] = send_kv[p]
    qg[p] = send_qg[p]

    pl.semaphore_wait(barrier, HEADS * CHIPS)

    for dc in range(CHIPS):
        for dp in range(HEADS):
            if dc or dp:
                remote(
                    send_kv.at[peer_p(dp)], kv.at[0, dc, p], s1.at[dc], r1.at[dc],
                    (peer_p(dp), peer_chip(dc) * 2 + core),
                ).start()
    for dp in range(1, HEADS):
        remote(send_qg.at[peer_p(dp)], qg.at[p], s2.at[0], r2.at[0], (peer_p(dp), g)).start()

    for load in loads[4:]:
        load.wait()
    length = lens_in[0]

    def scores(keys, values, q, gr, mask, e_ref, d_ref, rows, qs, qn):
        mx = jnp.full((8, qn), NEG, F)
        for c, r in enumerate(rows):
            s = nt(keys(c), q)
            keep = mask(c)
            if keep is not None:
                s = jnp.where(keep, s, NEG)
            sbuf[c % 4 * CB : c % 4 * CB + CB, c // 4 * qn : c // 4 * qn + qn] = s
            mx = jnp.maximum(mx, fold(s, jnp.max))
        m = rowmax(mx) * SCALE2
        l = jnp.zeros((8, qn), F)
        w = jnp.zeros((8, qn), F)
        for c, r in enumerate(rows):
            e = jnp.exp2(sbuf[c % 4 * CB : c % 4 * CB + CB, c // 4 * qn : c // 4 * qn + qn] * SCALE2 - m)
            e_ref[r, qs] = e.astype(B)
            dp = nt(values(c), gr).astype(B)
            d_ref[r, qs] = dp
            l = l + fold(e, jnp.sum)
            w = w + fold(e * dp.astype(F), jnp.sum)
        return m, rowsum(l), rowsum(w)

    def grads(rows, qs, factor, delta, e_ref, d_ref):
        low = factor.astype(B)
        for r in rows:
            probs = e_ref[r, qs] * low
            e_ref[r, qs] = probs
            d_ref[r, qs] = probs * (d_ref[r, qs].astype(F) - delta).astype(B)

    diagonal = lax.broadcasted_iota(jnp.int32, (CB, CB), 0) <= lax.broadcasted_iota(jnp.int32, (CB, CB), 1)

    def cont_rows(i):
        return [slice(j * CB, (j + 1) * CB) for j in range(i + 1)]

    def cont_scores(i):
        rows = cont_rows(i)
        qs = rows[i]
        m, l, w = scores(
            lambda c: k_c[rows[c], :], lambda c: v_c[rows[c], :], q_all[qs, :], g_all[qs, :],
            lambda c: diagonal if c == i else None, e_c, d_c, rows, qs, CB,
        )
        stat[0, 0:1, qs] = m
        stat[0, 1:2, qs] = l
        stat[0, 2:3, qs] = w

    for i in range(NC // CB):
        cont_scores(i)

    forwards = []

    def forward(dc):
        at = kv.at[0, dc]
        whole = at if dc else kv.at[0, 0, 0 : HEADS - 1]
        remote(whole, whole, s1.at[dc], r1.at[dc], (p, sibling)).wait()
        c = remote(at, kv.at[1, dc], s3.at[dc], r3.at[dc], (p, sibling))
        c.start()
        forwards.append(c)

    def kv_rows(which, r):
        first = r.start // HS
        return kv[first // CHIPS, first % CHIPS : first % CHIPS + CB // HS, :, which].reshape(CB, HS)

    groups = {1: (0, GK // 2), 2: (GK // 2, GK), 3: (GK, NP)}
    own_rows = slice(NC, NQ)

    def group_rows(k):
        return [slice(r, r + CB) for r in range(groups[k][0], groups[k][1], CB)]

    def prompt_scores(k, qs, qn, mask):
        rows = group_rows(k)
        m, l, w = scores(
            lambda c: kv_rows(0, rows[c]), lambda c: kv_rows(1, rows[c]), q_all[qs, :], g_all[qs, :],
            lambda c: mask(rows[c]), e_p, d_p, rows, qs, qn,
        )
        stat[k, 0:1, qs] = m
        stat[k, 1:2, qs] = l
        stat[k, 2:3, qs] = w

    def member_scores(k):
        def body(i, carry):
            prompt_scores(k, pl.ds(pl.multiple_of(i * WB, WB), WB), WB, lambda r: None)
            return carry

        lax.fori_loop(0, NC // WB, body, 0)

    def prompt_mask(r):
        row = lax.broadcasted_iota(jnp.int32, (CB, 1), 0)
        key_chip = chip + CHIPS - (r.start % GK // HS + row // HS)
        key_chip = jnp.where(key_chip >= CHIPS, key_chip - CHIPS, key_chip)
        key_group = key_chip * 2 + (other if r.start >= GK else core)
        key_pos = ((row % HS) // 16) * 256 + key_group * 16 + row % 16
        col = lax.broadcasted_iota(jnp.int32, (1, PQ), 1)
        query_pos = (col // 16) * 256 + g * 16 + col % 16
        return key_pos <= query_pos

    for dc in range(CHIPS // 2):
        forward(dc)
    member_scores(1)
    for dc in range(CHIPS // 2, CHIPS):
        forward(dc)
    member_scores(2)
    seven = qg.at[0 : HEADS - 1]
    remote(seven, seven, s2.at[0], r2.at[0], (p, sibling)).wait()
    q_all[own_rows, :] = qg[:, 0].reshape(PQ, HS)
    g_all[own_rows, :] = qg[:, 1].reshape(PQ, HS)
    prompt_scores(1, own_rows, PQ, prompt_mask)
    prompt_scores(2, own_rows, PQ, prompt_mask)
    for f in forwards:
        f.wait_recv()
    member_scores(3)
    prompt_scores(3, own_rows, PQ, prompt_mask)

    stat[0, 0:1, own_rows] = jnp.full((1, PQ), NEG, F)
    stat[0, 1:3, own_rows] = jnp.zeros((2, PQ), F)
    for i in range(NQ // PQ):
        qs = slice(i * PQ, (i + 1) * PQ)
        ms = [stat[k, 0:1, qs] for k in range(4)]
        top = jnp.maximum(jnp.maximum(ms[0], ms[1]), jnp.maximum(ms[2], ms[3]))
        scale = [jnp.exp2(m - top) for m in ms]
        l = sum(scale[k] * stat[k, 1:2, qs] for k in range(4))
        w = sum(scale[k] * stat[k, 2:3, qs] for k in range(4))
        inv = 1.0 / l
        delta = w * inv
        if i < NC // PQ:
            live = (lax.broadcasted_iota(jnp.int32, (1, PQ), 1) + i * PQ) < length
            inv = jnp.where(live, inv, 0.0)
        for k in range(4):
            stat[k, 3:4, qs] = scale[k] * inv
        stat[0, 4:5, qs] = delta

    def prompt_grads(k):
        def body(i, carry):
            qs = pl.ds(pl.multiple_of(i * WB, WB), WB)
            grads(group_rows(k), qs, stat[k, 3:4, qs], stat[0, 4:5, qs], e_p, d_p)
            return carry

        lax.fori_loop(0, NC // WB, body, 0)
        grads(group_rows(k), own_rows, stat[k, 3:4, own_rows], stat[0, 4:5, own_rows], e_p, d_p)

    def parts(start, size):
        r = slice(start, start + size)
        return nn(d_p[r, :], q_all[...]) * SCALE, nn(e_p[r, :], g_all[...])

    units = 4
    unit = GK // units
    prompt_grads(3)
    to_sibling = []
    for u in range(units):
        dk, dv = parts(GK + u * unit, unit)
        st_sib[u, 0] = dk.astype(B)
        st_sib[u, 1] = dv.astype(B)
        c = remote(st_sib.at[u], r_sib.at[u], s4.at[u], r4.at[u], (p, sibling))
        c.start()
        to_sibling.append(c)
    prompt_grads(1)
    prompt_grads(2)
    slot = p * CHIPS + chip
    per = CHIPS // units
    for u in range(units):
        dk, dv = parts(u * unit, unit)
        to_sibling[u].wait_recv()
        at = slice(u * per, (u + 1) * per)
        st_own[at, :, 0] = (dk + r_sib[u, 0].astype(F)).astype(B).reshape(per, HEADS, 16, HS)
        st_own[at, :, 1] = (dv + r_sib[u, 1].astype(F)).astype(B).reshape(per, HEADS, 16, HS)
        for dc in range(u * per, (u + 1) * per):
            for dp in range(HEADS):
                if dc or dp:
                    remote(
                        st_own.at[dc, peer_p(dp)], r_own.at[slot], s5.at[0], r5.at[0],
                        (peer_p(dp), back_chip(dc) * 2 + core),
                    ).start()
    r_own[slot] = st_own[0, p]

    for start in range(0, NP, CB):
        r = slice(start, start + CB)
        kt_p[:, r] = kv_rows(0, r).T
    dq = nn(kt_p[...], d_p[:, own_rows]) * SCALE
    dq_out[...] = dq.T.astype(B).reshape(HEADS, 16, HS)
    for dp in range(1, HEADS):
        remote(dq_out.at[peer_p(dp)], dq_in.at[p], s6.at[0], r6.at[0], (peer_p(dp), g)).start()
    dq_in[p] = dq_out[p]

    kt_c[...] = k_c[...].T
    for i in range(NC // CB):
        qs = slice(i * CB, (i + 1) * CB)
        grads(cont_rows(i), qs, stat[0, 3:4, qs], stat[0, 4:5, qs], e_c, d_c)

    for i in range(NC // QB):
        qs = slice(i * QB, (i + 1) * QB)
        first = slice(i * QB, i * QB + CB)
        second = slice(i * QB + CB, (i + 1) * QB)
        dq = nn(kt_p[...], d_p[:, qs])
        if i:
            dq = dq + nn(kt_c[:, 0 : i * QB], d_c[0 : i * QB, qs])
        left = nn(kt_c[:, first], d_c[first, first])
        right = nn(kt_c[:, i * QB : (i + 1) * QB], d_c[i * QB : (i + 1) * QB, second])
        dq = (dq + jnp.concatenate([left, right], axis=1)) * SCALE
        o_dq[0, qs, :] = dq.astype(B).T

    for j in range(NC // CB):
        r = slice(j * CB, (j + 1) * CB)
        qs = slice(j * CB, NC)
        o_dk[0, r, :] = (nn(d_c[r, qs], q_all[qs, :]) * SCALE).astype(B)
        o_dv[0, r, :] = nn(e_c[r, qs], g_all[qs, :]).astype(B)

    seven = dq_in.at[0 : HEADS - 1]
    remote(seven, seven, s6.at[0], r6.at[0], (p, sibling)).wait()
    for h in range(HEADS):
        o_pdq[:, h * HS : (h + 1) * HS] = dq_in[h]

    arrived = r_own.at[0 : HEADS * CHIPS - 1]
    remote(arrived, arrived, s5.at[0], r5.at[0], (p, sibling)).wait()
    for h in range(HEADS):
        cols = slice(h * HS, (h + 1) * HS)
        total = jnp.sum(r_own[h * CHIPS : (h + 1) * CHIPS].astype(F), axis=0)
        o_pdk[:, cols] = total[0].astype(B)
        o_pdv[:, cols] = total[1].astype(B)

    for c in forwards:
        c.wait_send()
    for c in to_sibling:
        c.wait_send()


def hand_over(*refs):
    ins, outs, sem = refs[:6], refs[6:12], refs[12]
    copies = [pltpu.make_async_copy(a, b, sem.at[i]) for i, (a, b) in enumerate(zip(ins, outs))]
    for c in copies:
        c.start()
    for c in copies:
        c.wait()


def shards(prompt_q, prompt_k, prompt_v, prompt_grad, cont_q, cont_k, cont_v, cont_grad, lengths):
    vm = pl.BlockSpec(memory_space=pltpu.VMEM)
    hbm = pl.BlockSpec(memory_space=pltpu.HBM)
    dma = pltpu.SemaphoreType.DMA
    vmem = pltpu.VMEM
    shapes = [(16, HEADS * HS)] * 3 + [(1, NC, HS)] * 3
    results = pl.pallas_call(
        kernel,
        out_shape=[vmem(shape, B) for shape in shapes],
        in_specs=[hbm] * 9,
        out_specs=[vm] * 6,
        scratch_shapes=[
            vmem((NQ, HS), B),
            vmem((NC, HS), B),
            vmem((NC, HS), B),
            vmem((NQ, HS), B),
            vmem((4, 16, HEADS * HS), B),
            vmem((HS, NC), B),
            vmem((HS, NP), B),
            vmem((2, CHIPS, HEADS, 2, 16, HS), B),
            vmem((HEADS, 2, 16, HS), B),
            vmem((HEADS, 2, 16, HS), B),
            vmem((HEADS, 2, 16, HS), B),
            vmem((GK, WB), F),
            vmem((NP, NQ), B),
            vmem((NC, NC), B),
            vmem((NP, NQ), B),
            vmem((NC, NC), B),
            vmem((4, 8, NQ), F),
            vmem((4, 2, GK // 4, HS), B),
            vmem((4, 2, GK // 4, HS), B),
            vmem((CHIPS, HEADS, 2, 16, HS), B),
            vmem((HEADS * CHIPS, 2, 16, HS), B),
            vmem((HEADS, 16, HS), B),
            vmem((HEADS, 16, HS), B),
            pltpu.SMEM((1,), jnp.int32),
            dma((9,)),
            dma((CHIPS,)),
            dma((CHIPS,)),
            dma((1,)),
            dma((1,)),
            dma((CHIPS,)),
            dma((CHIPS,)),
            dma((4,)),
            dma((4,)),
        ]
        + [dma((1,))] * 4,
        compiler_params=pltpu.CompilerParams(
            collective_id=0, has_side_effects=True, vmem_limit_bytes=58 * 2**20
        ),
    )(prompt_q, prompt_k, prompt_v, prompt_grad, cont_q, cont_k, cont_v, cont_grad, lengths)
    return pl.pallas_call(
        hand_over,
        out_shape=[jax.ShapeDtypeStruct(shape, B) for shape in shapes],
        in_specs=[vm] * 6,
        out_specs=[hbm] * 6,
        scratch_shapes=[dma((6,))],
    )(*[pltpu.with_memory_space_constraint(x, pltpu.VMEM) for x in results])


def solution(mesh):
    rows = P(("prompt", "group"), None)
    member = P("group", None, "prompt")
    return jax.shard_map(
        shards,
        mesh=mesh,
        in_specs=(rows,) * 4 + (member,) * 4 + (P("group"),),
        out_specs=(rows,) * 3 + (member,) * 3,
        check_vma=False,
    )
```

```python
import functools
import math

import jax
import jax.numpy as jnp
from jax import lax
from jax.experimental import pallas as pl
from jax.experimental.pallas import tpu as pltpu
from jax.sharding import PartitionSpec as P

F = jnp.float32
B = jnp.bfloat16
HS = 128
NP = 2048
NC = 2048
CB = 256
QB = 512
WB = 1024
GK = NP // 2
PQ = 128
NQ = NC + PQ
HEADS = 8
CHIPS = 8
MESH = pl.DeviceIdType.MESH
SCALE = HS**-0.5
SCALE2 = SCALE * math.log2(math.e)
NEG = -1e30


def nt(a, b):
    return lax.dot_general(a, b, (((1,), (1,)), ((), ())), preferred_element_type=F)


def nn(a, b):
    return jnp.dot(a, b, preferred_element_type=F)


def fold(x, op):
    return op(x.reshape(x.shape[0] // 8, 8, x.shape[1]), axis=0)


def rowmax(x):
    return jnp.max(x, axis=0, keepdims=True)


def rowsum(x):
    return jnp.sum(x, axis=0, keepdims=True)


def kernel(
    pq, pk, pv, pg, cq, ck, cv, cg, lens,
    o_pdq, o_pdk, o_pdv, o_dq, o_dk, o_dv,
    q_all, k_c, v_c, g_all, rows_in, kt_c, kt_p, kv, qg, send_kv, send_qg,
    q_two, sbuf, e_p, e_c, d_p, d_c, stat,
    st_sib, r_sib, st_own, r_own, dq_out, dq_in,
    lens_in, in_sem, s1, r1, s2, r2, s3, r3, s4, r4, s5, r5, s6, r6,
):
    p = lax.axis_index("prompt")
    g = lax.axis_index("group")
    core = lax.rem(g, 2)
    other = 1 - core
    chip = g // 2
    sibling = chip * 2 + other

    def peer_p(d):
        return lax.rem(p + d, HEADS)

    def peer_chip(d):
        return lax.rem(chip + d, CHIPS)

    def back_chip(d):
        return lax.rem(chip + CHIPS - d, CHIPS)

    def remote(src, dst, ssem, rsem, dev):
        return pltpu.make_async_remote_copy(
            src_ref=src, dst_ref=dst, send_sem=ssem, recv_sem=rsem, device_id=dev, device_id_type=MESH
        )

    loads = [
        pltpu.make_async_copy(src, dst, in_sem.at[i])
        for i, (src, dst) in enumerate(
            (
                (pk, rows_in.at[0]), (pv, rows_in.at[1]), (pq, rows_in.at[2]), (pg, rows_in.at[3]),
                (ck.at[0], k_c), (cq.at[0], q_all.at[0:NC]), (cv.at[0], v_c), (cg.at[0], g_all.at[0:NC]),
                (lens, lens_in),
            )
        )
    ]
    for load in loads:
        load.start()

    barrier = pltpu.get_barrier_semaphore()
    for dc in range(CHIPS):
        for dp in range(HEADS):
            if dc or dp:
                pl.semaphore_signal(
                    barrier, inc=1, device_id=(peer_p(dp), peer_chip(dc) * 2 + core), device_id_type=MESH
                )
    pl.semaphore_signal(barrier, inc=1, device_id=(p, sibling), device_id_type=MESH)

    for load in loads[:4]:
        load.wait()
    for h in range(HEADS):
        cols = slice(h * HS, (h + 1) * HS)
        send_kv[h, 0] = rows_in[0, :, cols]
        send_kv[h, 1] = rows_in[1, :, cols]
        send_qg[h, 0] = rows_in[2, :, cols]
        send_qg[h, 1] = rows_in[3, :, cols]
    kv[0, 0, p] = send_kv[p]
    qg[p] = send_qg[p]

    pl.semaphore_wait(barrier, HEADS * CHIPS)

    for dc in range(CHIPS):
        for dp in range(HEADS):
            if dc or dp:
                remote(
                    send_kv.at[peer_p(dp)], kv.at[0, dc, p], s1.at[dc], r1.at[dc],
                    (peer_p(dp), peer_chip(dc) * 2 + core),
                ).start()
    for dp in range(1, HEADS):
        remote(send_qg.at[peer_p(dp)], qg.at[p], s2.at[0], r2.at[0], (peer_p(dp), g)).start()

    for load in loads[4:]:
        load.wait()
    length = lens_in[0, 0]

    def scores(keys, values, q, gr, mask, e_ref, d_ref, rows, qs, qn):
        mx = jnp.full((8, qn), NEG, F)
        for c, r in enumerate(rows):
            k = keys(c)
            s = nt(jnp.concatenate([k, k], axis=1), q)
            keep = mask(c)
            if keep is not None:
                s = jnp.where(keep, s, NEG)
            sbuf[c % 4 * CB : c % 4 * CB + CB, c // 4 * qn : c // 4 * qn + qn] = s
            mx = jnp.maximum(mx, fold(s, jnp.max))
        m = rowmax(mx)
        l = jnp.zeros((8, qn), F)
        w = jnp.zeros((8, qn), F)
        for c, r in enumerate(rows):
            e = jnp.exp2(sbuf[c % 4 * CB : c % 4 * CB + CB, c // 4 * qn : c // 4 * qn + qn] - m)
            e_ref[r, qs] = e.astype(B)
            dp = nt(values(c), gr).astype(B)
            d_ref[r, qs] = dp
            l = l + fold(e, jnp.sum)
            w = w + fold(e * dp.astype(F), jnp.sum)
        return m, rowsum(l), rowsum(w)

    def grads(rows, qs, factor, delta, e_ref, d_ref):
        low = factor.astype(B)
        for r in rows:
            probs = e_ref[r, qs] * low
            e_ref[r, qs] = probs
            d_ref[r, qs] = probs * (d_ref[r, qs].astype(F) - delta).astype(B)

    diagonal = lax.broadcasted_iota(jnp.int32, (CB, CB), 0) <= lax.broadcasted_iota(jnp.int32, (CB, CB), 1)

    def split_scaled(rows):
        scaled = q_all[rows, :].astype(F) * SCALE2
        high = scaled.astype(B)
        q_two[rows, 0:HS] = high
        q_two[rows, HS:] = (scaled - high.astype(F)).astype(B)

    split_scaled(slice(0, NC))

    def cont_rows(i):
        return [slice(j * CB, (j + 1) * CB) for j in range(i + 1)]

    def cont_scores(i):
        rows = cont_rows(i)
        qs = rows[i]
        m, l, w = scores(
            lambda c: k_c[rows[c], :], lambda c: v_c[rows[c], :], q_two[qs, :], g_all[qs, :],
            lambda c: diagonal if c == i else None, e_c, d_c, rows, qs, CB,
        )
        stat[0, 0:1, qs] = m
        stat[0, 1:2, qs] = l
        stat[0, 2:3, qs] = w

    for i in range(NC // CB):
        cont_scores(i)

    forwards = []

    def forward(dc):
        at = kv.at[0, dc]
        whole = at if dc else kv.at[0, 0, 0 : HEADS - 1]
        remote(whole, whole, s1.at[dc], r1.at[dc], (p, sibling)).wait()
        c = remote(at, kv.at[1, dc], s3.at[dc], r3.at[dc], (p, sibling))
        c.start()
        forwards.append(c)

    def kv_rows(which, r):
        first = r.start // HS
        return kv[first // CHIPS, first % CHIPS : first % CHIPS + CB // HS, :, which].reshape(CB, HS)

    groups = {1: (0, GK // 2), 2: (GK // 2, GK), 3: (GK, NP)}
    own_rows = slice(NC, NQ)

    def group_rows(k):
        return [slice(r, r + CB) for r in range(groups[k][0], groups[k][1], CB)]

    def prompt_scores(k, qs, qn, mask):
        rows = group_rows(k)
        m, l, w = scores(
            lambda c: kv_rows(0, rows[c]), lambda c: kv_rows(1, rows[c]), q_two[qs, :], g_all[qs, :],
            lambda c: mask(rows[c]), e_p, d_p, rows, qs, qn,
        )
        stat[k, 0:1, qs] = m
        stat[k, 1:2, qs] = l
        stat[k, 2:3, qs] = w

    def member_scores(k):
        def body(i, carry):
            prompt_scores(k, pl.ds(pl.multiple_of(i * WB, WB), WB), WB, lambda r: None)
            return carry

        lax.fori_loop(0, NC // WB, body, 0)

    def prompt_mask(r):
        row = lax.broadcasted_iota(jnp.int32, (CB, 1), 0)
        key_chip = chip + CHIPS - (r.start % GK // HS + row // HS)
        key_chip = jnp.where(key_chip >= CHIPS, key_chip - CHIPS, key_chip)
        key_group = key_chip * 2 + (other if r.start >= GK else core)
        key_pos = ((row % HS) // 16) * 256 + key_group * 16 + row % 16
        col = lax.broadcasted_iota(jnp.int32, (1, PQ), 1)
        query_pos = (col // 16) * 256 + g * 16 + col % 16
        return key_pos <= query_pos

    for dc in range(CHIPS // 2):
        forward(dc)
    member_scores(1)
    for dc in range(CHIPS // 2, CHIPS):
        forward(dc)
    member_scores(2)
    seven = qg.at[0 : HEADS - 1]
    remote(seven, seven, s2.at[0], r2.at[0], (p, sibling)).wait()
    q_all[own_rows, :] = qg[:, 0].reshape(PQ, HS)
    g_all[own_rows, :] = qg[:, 1].reshape(PQ, HS)
    split_scaled(own_rows)
    prompt_scores(1, own_rows, PQ, prompt_mask)
    prompt_scores(2, own_rows, PQ, prompt_mask)
    for f in forwards:
        f.wait_recv()
    member_scores(3)
    prompt_scores(3, own_rows, PQ, prompt_mask)

    stat[0, 0:1, own_rows] = jnp.full((1, PQ), NEG, F)
    stat[0, 1:3, own_rows] = jnp.zeros((2, PQ), F)
    for i in range(NQ // PQ):
        qs = slice(i * PQ, (i + 1) * PQ)
        ms = [stat[k, 0:1, qs] for k in range(4)]
        top = jnp.maximum(jnp.maximum(ms[0], ms[1]), jnp.maximum(ms[2], ms[3]))
        scale = [jnp.exp2(m - top) for m in ms]
        l = sum(scale[k] * stat[k, 1:2, qs] for k in range(4))
        w = sum(scale[k] * stat[k, 2:3, qs] for k in range(4))
        inv = 1.0 / l
        delta = w * inv
        if i < NC // PQ:
            live = (lax.broadcasted_iota(jnp.int32, (1, PQ), 1) + i * PQ) < length
            inv = jnp.where(live, inv, 0.0)
        for k in range(4):
            stat[k, 3:4, qs] = scale[k] * inv
        stat[0, 4:5, qs] = delta

    def prompt_grads(k):
        def body(i, carry):
            qs = pl.ds(pl.multiple_of(i * WB, WB), WB)
            grads(group_rows(k), qs, stat[k, 3:4, qs], stat[0, 4:5, qs], e_p, d_p)
            return carry

        lax.fori_loop(0, NC // WB, body, 0)
        grads(group_rows(k), own_rows, stat[k, 3:4, own_rows], stat[0, 4:5, own_rows], e_p, d_p)

    def parts(start, size):
        r = slice(start, start + size)
        return nn(d_p[r, :], q_all[...]) * SCALE, nn(e_p[r, :], g_all[...])

    halves = 2
    units = 4
    unit = GK // units
    prompt_grads(3)
    to_sibling = []
    for u in range(halves):
        dk, dv = parts(GK + u * 2 * unit, 2 * unit)
        st_sib[u, 0] = dk.astype(B)
        st_sib[u, 1] = dv.astype(B)
        c = remote(st_sib.at[u], r_sib.at[u], s4.at[u], r4.at[u], (p, sibling))
        c.start()
        to_sibling.append(c)
    prompt_grads(1)
    prompt_grads(2)
    slot = p * CHIPS + chip
    per = CHIPS // units
    for u in range(units):
        dk, dv = parts(u * unit, unit)
        if u % 2 == 0:
            to_sibling[u // 2].wait_recv()
        at = slice(u * per, (u + 1) * per)
        share = slice(u % 2 * unit, u % 2 * unit + unit)
        st_own[at, :, 0] = (dk + r_sib[u // 2, 0, share].astype(F)).astype(B).reshape(per, HEADS, 16, HS)
        st_own[at, :, 1] = (dv + r_sib[u // 2, 1, share].astype(F)).astype(B).reshape(per, HEADS, 16, HS)
        for dc in range(u * per, (u + 1) * per):
            for dp in range(HEADS):
                if dc or dp:
                    remote(
                        st_own.at[dc, peer_p(dp)], r_own.at[slot], s5.at[0], r5.at[0],
                        (peer_p(dp), back_chip(dc) * 2 + core),
                    ).start()
    r_own[slot] = st_own[0, p]

    for start in range(0, NP, CB):
        r = slice(start, start + CB)
        kt_p[:, r] = kv_rows(0, r).T
    dq = nn(kt_p[...], d_p[:, own_rows]) * SCALE
    dq_out[...] = dq.T.astype(B).reshape(HEADS, 16, HS)
    for dp in range(1, HEADS):
        remote(dq_out.at[peer_p(dp)], dq_in.at[p], s6.at[0], r6.at[0], (peer_p(dp), g)).start()
    dq_in[p] = dq_out[p]

    kt_c[...] = k_c[...].T
    for i in range(NC // CB):
        qs = slice(i * CB, (i + 1) * CB)
        grads(cont_rows(i), qs, stat[0, 3:4, qs], stat[0, 4:5, qs], e_c, d_c)

    for i in range(NC // QB):
        qs = slice(i * QB, (i + 1) * QB)
        first = slice(i * QB, i * QB + CB)
        second = slice(i * QB + CB, (i + 1) * QB)
        dq = nn(kt_p[...], d_p[:, qs])
        if i:
            dq = dq + nn(kt_c[:, 0 : i * QB], d_c[0 : i * QB, qs])
        left = nn(kt_c[:, first], d_c[first, first])
        right = nn(kt_c[:, i * QB : (i + 1) * QB], d_c[i * QB : (i + 1) * QB, second])
        dq = (dq + jnp.concatenate([left, right], axis=1)) * SCALE
        o_dq[0, qs, :] = dq.astype(B).T

    for j in range(NC // CB):
        r = slice(j * CB, (j + 1) * CB)
        qs = slice(j * CB, NC)
        o_dk[0, r, :] = (nn(d_c[r, qs], q_all[qs, :]) * SCALE).astype(B)
        o_dv[0, r, :] = nn(e_c[r, qs], g_all[qs, :]).astype(B)

    seven = dq_in.at[0 : HEADS - 1]
    remote(seven, seven, s6.at[0], r6.at[0], (p, sibling)).wait()
    for h in range(HEADS):
        o_pdq[:, h * HS : (h + 1) * HS] = dq_in[h]

    arrived = r_own.at[0 : HEADS * CHIPS - 1]
    remote(arrived, arrived, s5.at[0], r5.at[0], (p, sibling)).wait()
    for h in range(HEADS):
        cols = slice(h * HS, (h + 1) * HS)
        total = jnp.sum(r_own[h * CHIPS : (h + 1) * CHIPS].astype(F), axis=0)
        o_pdk[:, cols] = total[0].astype(B)
        o_pdv[:, cols] = total[1].astype(B)

    for c in forwards:
        c.wait_send()
    for c in to_sibling:
        c.wait_send()


def hand_over(*refs):
    ins, outs, sem = refs[:6], refs[6:12], refs[12]
    copies = [pltpu.make_async_copy(a, b, sem.at[i]) for i, (a, b) in enumerate(zip(ins, outs))]
    for c in copies:
        c.start()
    for c in copies:
        c.wait()


def shards(prompt_q, prompt_k, prompt_v, prompt_grad, cont_q, cont_k, cont_v, cont_grad, lengths):
    vm = pl.BlockSpec(memory_space=pltpu.VMEM)
    hbm = pl.BlockSpec(memory_space=pltpu.HBM)
    dma = pltpu.SemaphoreType.DMA
    vmem = pltpu.VMEM
    shapes = [(16, HEADS * HS)] * 3 + [(1, NC, HS)] * 3
    results = pl.pallas_call(
        kernel,
        out_shape=[vmem(shape, B) for shape in shapes],
        in_specs=[hbm] * 9,
        out_specs=[vm] * 6,
        scratch_shapes=[
            vmem((NQ, HS), B),
            vmem((NC, HS), B),
            vmem((NC, HS), B),
            vmem((NQ, HS), B),
            vmem((4, 16, HEADS * HS), B),
            vmem((HS, NC), B),
            vmem((HS, NP), B),
            vmem((2, CHIPS, HEADS, 2, 16, HS), B),
            vmem((HEADS, 2, 16, HS), B),
            vmem((HEADS, 2, 16, HS), B),
            vmem((HEADS, 2, 16, HS), B),
            vmem((NQ, 2 * HS), B),
            vmem((GK, WB), F),
            vmem((NP, NQ), B),
            vmem((NC, NC), B),
            vmem((NP, NQ), B),
            vmem((NC, NC), B),
            vmem((4, 8, NQ), F),
            vmem((2, 2, GK // 2, HS), B),
            vmem((2, 2, GK // 2, HS), B),
            vmem((CHIPS, HEADS, 2, 16, HS), B),
            vmem((HEADS * CHIPS, 2, 16, HS), B),
            vmem((HEADS, 16, HS), B),
            vmem((HEADS, 16, HS), B),
            pltpu.SMEM((1, 1), jnp.int32),
            dma((9,)),
            dma((CHIPS,)),
            dma((CHIPS,)),
            dma((1,)),
            dma((1,)),
            dma((CHIPS,)),
            dma((CHIPS,)),
            dma((2,)),
            dma((2,)),
        ]
        + [dma((1,))] * 4,
        compiler_params=pltpu.CompilerParams(
            collective_id=0, has_side_effects=True, vmem_limit_bytes=58 * 2**20
        ),
    )(prompt_q, prompt_k, prompt_v, prompt_grad, cont_q, cont_k, cont_v, cont_grad, lengths.reshape(1, 1))
    return pl.pallas_call(
        hand_over,
        out_shape=[jax.ShapeDtypeStruct(shape, B) for shape in shapes],
        in_specs=[vm] * 6,
        out_specs=[hbm] * 6,
        scratch_shapes=[dma((6,))],
    )(*[pltpu.with_memory_space_constraint(x, pltpu.VMEM) for x in results])


def solution(mesh):
    rows = P(("prompt", "group"), None)
    member = P("group", None, "prompt")
    return jax.shard_map(
        shards,
        mesh=mesh,
        in_specs=(rows,) * 4 + (member,) * 4 + (P("group"),),
        out_specs=(rows,) * 3 + (member,) * 3,
        check_vma=False,
    )
```

```python
import functools
import math

import jax
import jax.numpy as jnp
from jax import lax
from jax.experimental import pallas as pl
from jax.experimental.pallas import tpu as pltpu
from jax.sharding import PartitionSpec as P

F = jnp.float32
B = jnp.bfloat16
HS = 128
NP = 2048
NC = 2048
CB = 256
QB = 512
WB = 1024
GK = NP // 2
PQ = 128
NQ = NC + PQ
HEADS = 8
CHIPS = 8
MESH = pl.DeviceIdType.MESH
SCALE = HS**-0.5
SCALE2 = SCALE * math.log2(math.e)
NEG = -1e30


def nt(a, b):
    return lax.dot_general(a, b, (((1,), (1,)), ((), ())), preferred_element_type=F)


def nn(a, b):
    return jnp.dot(a, b, preferred_element_type=F)


def fold(x, op):
    return op(x.reshape(x.shape[0] // 8, 8, x.shape[1]), axis=0)


def rowmax(x):
    return jnp.max(x, axis=0, keepdims=True)


def rowsum(x):
    return jnp.sum(x, axis=0, keepdims=True)


def kernel(
    pq, pk, pv, pg, cq, ck, cv, cg, lens,
    o_pdq, o_pdk, o_pdv, o_dq, o_dk, o_dv,
    q_all, k_c, v_c, g_all, rows_in, kt_c, kt_p, kv, qg, send_kv, send_qg,
    q_two, sbuf, e_p, e_c, d_p, d_c, stat,
    st_sib, r_sib, st_own, r_own, dq_out, dq_in,
    lens_in, in_sem, s1, r1, s2, r2, s3, r3, s4, r4, s5, r5, s6, r6,
):
    p = lax.axis_index("prompt")
    g = lax.axis_index("group")
    core = lax.rem(g, 2)
    other = 1 - core
    chip = g // 2
    sibling = chip * 2 + other

    def peer_p(d):
        return lax.rem(p + d, HEADS)

    def peer_chip(d):
        return lax.rem(chip + d, CHIPS)

    def back_chip(d):
        return lax.rem(chip + CHIPS - d, CHIPS)

    def remote(src, dst, ssem, rsem, dev):
        return pltpu.make_async_remote_copy(
            src_ref=src, dst_ref=dst, send_sem=ssem, recv_sem=rsem, device_id=dev, device_id_type=MESH
        )

    loads = [
        pltpu.make_async_copy(src, dst, in_sem.at[i])
        for i, (src, dst) in enumerate(
            (
                (pk, rows_in.at[0]), (pv, rows_in.at[1]), (pq, rows_in.at[2]), (pg, rows_in.at[3]),
                (ck.at[0], k_c), (cq.at[0], q_all.at[0:NC]), (cv.at[0], v_c), (cg.at[0], g_all.at[0:NC]),
                (lens, lens_in),
            )
        )
    ]
    for load in loads:
        load.start()

    barrier = pltpu.get_barrier_semaphore()
    for dc in range(CHIPS):
        for dp in range(HEADS):
            if dc or dp:
                pl.semaphore_signal(
                    barrier, inc=1, device_id=(peer_p(dp), peer_chip(dc) * 2 + core), device_id_type=MESH
                )
    pl.semaphore_signal(barrier, inc=1, device_id=(p, sibling), device_id_type=MESH)

    for load in loads[:4]:
        load.wait()
    for h in range(HEADS):
        cols = slice(h * HS, (h + 1) * HS)
        send_kv[h, 0] = rows_in[0, :, cols]
        send_kv[h, 1] = rows_in[1, :, cols]
        send_qg[h, 0] = rows_in[2, :, cols]
        send_qg[h, 1] = rows_in[3, :, cols]
    kv[0, 0, p] = send_kv[p]
    qg[p] = send_qg[p]

    pl.semaphore_wait(barrier, HEADS * CHIPS)

    for dc in range(CHIPS):
        for dp in range(HEADS):
            if dc or dp:
                remote(
                    send_kv.at[peer_p(dp)], kv.at[0, dc, p], s1.at[dc], r1.at[dc],
                    (peer_p(dp), peer_chip(dc) * 2 + core),
                ).start()
    for dp in range(1, HEADS):
        remote(send_qg.at[peer_p(dp)], qg.at[p], s2.at[0], r2.at[0], (peer_p(dp), g)).start()

    for load in loads[4:]:
        load.wait()
    length = lens_in[0, 0]

    def place(c, qn):
        return slice(c % 4 * CB, c % 4 * CB + CB), slice(c // 4 * qn, c // 4 * qn + qn)

    def scores(keys, values, q, gr, mask, e_ref, d_ref, rows, qs, qn):
        mx = jnp.full((8, qn), NEG, F)
        for c, r in enumerate(rows):
            k = keys(c)
            s = nt(jnp.concatenate([k, k], axis=1), q)
            keep = mask(c)
            if keep is not None:
                s = jnp.where(keep, s, NEG)
            sbuf[place(c, qn)] = s
            mx = jnp.maximum(mx, fold(s, jnp.max))
        m = rowmax(mx)
        l = jnp.zeros((8, qn), F)
        w = jnp.zeros((8, qn), F)
        for c, r in enumerate(rows):
            e = jnp.exp2(sbuf[place(c, qn)] - m)
            e_ref[r, qs] = e.astype(B)
            dp = nt(values(c), gr).astype(B)
            d_ref[r, qs] = dp
            l = l + fold(e, jnp.sum)
            w = w + fold(e * dp.astype(F), jnp.sum)
        return m, rowsum(l), rowsum(w)

    def grads(rows, qs, factor, delta, e_ref, d_ref):
        low = factor.astype(B)
        for r in rows:
            probs = e_ref[r, qs] * low
            e_ref[r, qs] = probs
            d_ref[r, qs] = probs * (d_ref[r, qs].astype(F) - delta).astype(B)

    diagonal = lax.broadcasted_iota(jnp.int32, (CB, CB), 0) <= lax.broadcasted_iota(jnp.int32, (CB, CB), 1)

    def split_scaled(rows):
        scaled = q_all[rows, :].astype(F) * SCALE2
        high = scaled.astype(B)
        q_two[rows, 0:HS] = high
        q_two[rows, HS:] = (scaled - high.astype(F)).astype(B)

    split_scaled(slice(0, NC))

    def cont_rows(i):
        return [slice(j * CB, (j + 1) * CB) for j in range(i + 1)]

    def cont_scores(i):
        rows = cont_rows(i)
        qs = rows[i]
        m, l, w = scores(
            lambda c: k_c[rows[c], :], lambda c: v_c[rows[c], :], q_two[qs, :], g_all[qs, :],
            lambda c: diagonal if c == i else None, e_c, d_c, rows, qs, CB,
        )
        stat[0, 0:1, qs] = m
        stat[0, 1:2, qs] = l
        stat[0, 2:3, qs] = w

    for i in range(NC // CB):
        cont_scores(i)

    forwards = []

    def forward(dc):
        at = kv.at[0, dc]
        whole = at if dc else kv.at[0, 0, 0 : HEADS - 1]
        remote(whole, whole, s1.at[dc], r1.at[dc], (p, sibling)).wait()
        c = remote(at, kv.at[1, dc], s3.at[dc], r3.at[dc], (p, sibling))
        c.start()
        forwards.append(c)

    def kv_rows(which, r):
        first = r.start // HS
        return kv[first // CHIPS, first % CHIPS : first % CHIPS + CB // HS, :, which].reshape(CB, HS)

    groups = {k + 1: (k * GK // 2, (k + 1) * GK // 2) for k in range(4)}
    own_rows = slice(NC, NQ)

    def group_rows(k):
        return [slice(r, r + CB) for r in range(groups[k][0], groups[k][1], CB)]

    def prompt_scores(k, qs, qn, mask):
        rows = group_rows(k)
        m, l, w = scores(
            lambda c: kv_rows(0, rows[c]), lambda c: kv_rows(1, rows[c]), q_two[qs, :], g_all[qs, :],
            lambda c: mask(rows[c]), e_p, d_p, rows, qs, qn,
        )
        stat[k, 0:1, qs] = m
        stat[k, 1:2, qs] = l
        stat[k, 2:3, qs] = w

    def member_scores(k):
        def body(i, carry):
            prompt_scores(k, pl.ds(pl.multiple_of(i * WB, WB), WB), WB, lambda r: None)
            return carry

        lax.fori_loop(0, NC // WB, body, 0)

    def prompt_mask(r):
        row = lax.broadcasted_iota(jnp.int32, (CB, 1), 0)
        key_chip = chip + CHIPS - (r.start % GK // HS + row // HS)
        key_chip = jnp.where(key_chip >= CHIPS, key_chip - CHIPS, key_chip)
        key_group = key_chip * 2 + (other if r.start >= GK else core)
        key_pos = ((row % HS) // 16) * 256 + key_group * 16 + row % 16
        col = lax.broadcasted_iota(jnp.int32, (1, PQ), 1)
        query_pos = (col // 16) * 256 + g * 16 + col % 16
        return key_pos <= query_pos

    for dc in range(CHIPS // 2):
        forward(dc)
    member_scores(1)
    for dc in range(CHIPS // 2):
        forwards[dc].wait_recv()
    member_scores(3)
    for dc in range(CHIPS // 2, CHIPS):
        forward(dc)
    member_scores(2)
    seven = qg.at[0 : HEADS - 1]
    remote(seven, seven, s2.at[0], r2.at[0], (p, sibling)).wait()
    q_all[own_rows, :] = qg[:, 0].reshape(PQ, HS)
    g_all[own_rows, :] = qg[:, 1].reshape(PQ, HS)
    split_scaled(own_rows)
    for k in (1, 2, 3):
        prompt_scores(k, own_rows, PQ, prompt_mask)
    for dc in range(CHIPS // 2, CHIPS):
        forwards[dc].wait_recv()
    member_scores(4)
    prompt_scores(4, own_rows, PQ, prompt_mask)

    stat[0, 0:1, own_rows] = jnp.full((1, PQ), NEG, F)
    stat[0, 1:3, own_rows] = jnp.zeros((2, PQ), F)
    for i in range(NQ // PQ):
        qs = slice(i * PQ, (i + 1) * PQ)
        ms = [stat[k, 0:1, qs] for k in range(5)]
        top = ms[0]
        for m in ms[1:]:
            top = jnp.maximum(top, m)
        scale = [jnp.exp2(m - top) for m in ms]
        l = sum(scale[k] * stat[k, 1:2, qs] for k in range(5))
        w = sum(scale[k] * stat[k, 2:3, qs] for k in range(5))
        inv = 1.0 / l
        delta = w * inv
        if i < NC // PQ:
            live = (lax.broadcasted_iota(jnp.int32, (1, PQ), 1) + i * PQ) < length
            inv = jnp.where(live, inv, 0.0)
        for k in range(5):
            stat[k, 3:4, qs] = scale[k] * inv
        stat[0, 4:5, qs] = delta

    def prompt_grads(k):
        def body(i, carry):
            qs = pl.ds(pl.multiple_of(i * WB, WB), WB)
            grads(group_rows(k), qs, stat[k, 3:4, qs], stat[0, 4:5, qs], e_p, d_p)
            return carry

        lax.fori_loop(0, NC // WB, body, 0)
        grads(group_rows(k), own_rows, stat[k, 3:4, own_rows], stat[0, 4:5, own_rows], e_p, d_p)

    def parts(start, size):
        r = slice(start, start + size)
        return nn(d_p[r, :], q_all[...]) * SCALE, nn(e_p[r, :], g_all[...])

    halves = 2
    units = 4
    unit = GK // units
    prompt_grads(3)
    prompt_grads(4)
    to_sibling = []
    for u in range(halves):
        dk, dv = parts(GK + u * 2 * unit, 2 * unit)
        st_sib[u, 0] = dk.astype(B)
        st_sib[u, 1] = dv.astype(B)
        c = remote(st_sib.at[u], r_sib.at[u], s4.at[u], r4.at[u], (p, sibling))
        c.start()
        to_sibling.append(c)
    prompt_grads(1)
    prompt_grads(2)
    slot = p * CHIPS + chip
    per = CHIPS // units
    for u in range(units):
        dk, dv = parts(u * unit, unit)
        if u % 2 == 0:
            to_sibling[u // 2].wait_recv()
        at = slice(u * per, (u + 1) * per)
        share = slice(u % 2 * unit, u % 2 * unit + unit)
        st_own[at, :, 0] = (dk + r_sib[u // 2, 0, share].astype(F)).astype(B).reshape(per, HEADS, 16, HS)
        st_own[at, :, 1] = (dv + r_sib[u // 2, 1, share].astype(F)).astype(B).reshape(per, HEADS, 16, HS)
        for dc in range(u * per, (u + 1) * per):
            for dp in range(HEADS):
                if dc or dp:
                    remote(
                        st_own.at[dc, peer_p(dp)], r_own.at[slot], s5.at[0], r5.at[0],
                        (peer_p(dp), back_chip(dc) * 2 + core),
                    ).start()
    r_own[slot] = st_own[0, p]

    for start in range(0, NP, CB):
        r = slice(start, start + CB)
        kt_p[:, r] = kv_rows(0, r).T
    dq = nn(kt_p[...], d_p[:, own_rows]) * SCALE
    dq_out[...] = dq.T.astype(B).reshape(HEADS, 16, HS)
    for dp in range(1, HEADS):
        remote(dq_out.at[peer_p(dp)], dq_in.at[p], s6.at[0], r6.at[0], (peer_p(dp), g)).start()
    dq_in[p] = dq_out[p]

    kt_c[...] = k_c[...].T
    for i in range(NC // CB):
        qs = slice(i * CB, (i + 1) * CB)
        grads(cont_rows(i), qs, stat[0, 3:4, qs], stat[0, 4:5, qs], e_c, d_c)

    for i in range(NC // QB):
        qs = slice(i * QB, (i + 1) * QB)
        first = slice(i * QB, i * QB + CB)
        second = slice(i * QB + CB, (i + 1) * QB)
        dq = nn(kt_p[...], d_p[:, qs])
        if i:
            dq = dq + nn(kt_c[:, 0 : i * QB], d_c[0 : i * QB, qs])
        left = nn(kt_c[:, first], d_c[first, first])
        right = nn(kt_c[:, i * QB : (i + 1) * QB], d_c[i * QB : (i + 1) * QB, second])
        dq = (dq + jnp.concatenate([left, right], axis=1)) * SCALE
        o_dq[0, qs, :] = dq.astype(B).T

    for j in range(NC // CB):
        r = slice(j * CB, (j + 1) * CB)
        qs = slice(j * CB, NC)
        o_dk[0, r, :] = (nn(d_c[r, qs], q_all[qs, :]) * SCALE).astype(B)
        o_dv[0, r, :] = nn(e_c[r, qs], g_all[qs, :]).astype(B)

    seven = dq_in.at[0 : HEADS - 1]
    remote(seven, seven, s6.at[0], r6.at[0], (p, sibling)).wait()
    for h in range(HEADS):
        o_pdq[:, h * HS : (h + 1) * HS] = dq_in[h]

    arrived = r_own.at[0 : HEADS * CHIPS - 1]
    remote(arrived, arrived, s5.at[0], r5.at[0], (p, sibling)).wait()
    for h in range(HEADS):
        cols = slice(h * HS, (h + 1) * HS)
        total = jnp.sum(r_own[h * CHIPS : (h + 1) * CHIPS].astype(F), axis=0)
        o_pdk[:, cols] = total[0].astype(B)
        o_pdv[:, cols] = total[1].astype(B)

    for c in forwards:
        c.wait_send()
    for c in to_sibling:
        c.wait_send()


def hand_over(*refs):
    ins, outs, sem = refs[:6], refs[6:12], refs[12]
    copies = [pltpu.make_async_copy(a, b, sem.at[i]) for i, (a, b) in enumerate(zip(ins, outs))]
    for c in copies:
        c.start()
    for c in copies:
        c.wait()


def shards(prompt_q, prompt_k, prompt_v, prompt_grad, cont_q, cont_k, cont_v, cont_grad, lengths):
    vm = pl.BlockSpec(memory_space=pltpu.VMEM)
    hbm = pl.BlockSpec(memory_space=pltpu.HBM)
    dma = pltpu.SemaphoreType.DMA
    vmem = pltpu.VMEM
    shapes = [(16, HEADS * HS)] * 3 + [(1, NC, HS)] * 3
    results = pl.pallas_call(
        kernel,
        out_shape=[vmem(shape, B) for shape in shapes],
        in_specs=[hbm] * 9,
        out_specs=[vm] * 6,
        scratch_shapes=[
            vmem((NQ, HS), B),
            vmem((NC, HS), B),
            vmem((NC, HS), B),
            vmem((NQ, HS), B),
            vmem((4, 16, HEADS * HS), B),
            vmem((HS, NC), B),
            vmem((HS, NP), B),
            vmem((2, CHIPS, HEADS, 2, 16, HS), B),
            vmem((HEADS, 2, 16, HS), B),
            vmem((HEADS, 2, 16, HS), B),
            vmem((HEADS, 2, 16, HS), B),
            vmem((NQ, 2 * HS), B),
            vmem((GK, WB), F),
            vmem((NP, NQ), B),
            vmem((NC, NC), B),
            vmem((NP, NQ), B),
            vmem((NC, NC), B),
            vmem((5, 8, NQ), F),
            vmem((2, 2, GK // 2, HS), B),
            vmem((2, 2, GK // 2, HS), B),
            vmem((CHIPS, HEADS, 2, 16, HS), B),
            vmem((HEADS * CHIPS, 2, 16, HS), B),
            vmem((HEADS, 16, HS), B),
            vmem((HEADS, 16, HS), B),
            pltpu.SMEM((1, 1), jnp.int32),
            dma((9,)),
            dma((CHIPS,)),
            dma((CHIPS,)),
            dma((1,)),
            dma((1,)),
            dma((CHIPS,)),
            dma((CHIPS,)),
            dma((2,)),
            dma((2,)),
        ]
        + [dma((1,))] * 4,
        compiler_params=pltpu.CompilerParams(
            collective_id=0, has_side_effects=True, vmem_limit_bytes=60 * 2**20
        ),
    )(prompt_q, prompt_k, prompt_v, prompt_grad, cont_q, cont_k, cont_v, cont_grad, lengths.reshape(1, 1))
    return pl.pallas_call(
        hand_over,
        out_shape=[jax.ShapeDtypeStruct(shape, B) for shape in shapes],
        in_specs=[vm] * 6,
        out_specs=[hbm] * 6,
        scratch_shapes=[dma((6,))],
    )(*[pltpu.with_memory_space_constraint(x, pltpu.VMEM) for x in results])


def solution(mesh):
    rows = P(("prompt", "group"), None)
    member = P("group", None, "prompt")
    return jax.shard_map(
        shards,
        mesh=mesh,
        in_specs=(rows,) * 4 + (member,) * 4 + (P("group"),),
        out_specs=(rows,) * 3 + (member,) * 3,
        check_vma=False,
    )
```

```python
import functools
import math

import jax
import jax.numpy as jnp
from jax import lax
from jax.experimental import pallas as pl
from jax.experimental.pallas import tpu as pltpu
from jax.sharding import PartitionSpec as P

F = jnp.float32
B = jnp.bfloat16
HS = 128
NP = 2048
NC = 2048
CB = 256
QB = 512
WB = 1024
GK = NP // 2
PQ = 128
NQ = NC + PQ
HEADS = 8
CHIPS = 8
MESH = pl.DeviceIdType.MESH
SCALE = HS**-0.5
SCALE2 = SCALE * math.log2(math.e)
NEG = -1e30


def nt(a, b):
    return lax.dot_general(a, b, (((1,), (1,)), ((), ())), preferred_element_type=F)


def nn(a, b):
    return jnp.dot(a, b, preferred_element_type=F)


def fold(x, op):
    return op(x.reshape(x.shape[0] // 8, 8, x.shape[1]), axis=0)


def rowmax(x):
    return jnp.max(x, axis=0, keepdims=True)


def rowsum(x):
    return jnp.sum(x, axis=0, keepdims=True)


def kernel(
    pq, pk, pv, pg, cq, ck, cv, cg, lens,
    o_pdq, o_pdk, o_pdv, o_dq, o_dk, o_dv,
    q_all, k_c, v_c, g_all, rows_in, kt_c, kt_p, kv, qg, send_kv, send_qg,
    q_two, sbuf, e_p, e_c, d_p, d_c, stat,
    st_sib, r_sib, st_own, r_own, dq_out, dq_in,
    lens_in, in_sem, s1, r1, s2, r2, s3, r3, s4, r4, s5, r5, s6, r6,
):
    p = lax.axis_index("prompt")
    g = lax.axis_index("group")
    core = lax.rem(g, 2)
    other = 1 - core
    chip = g // 2
    sibling = chip * 2 + other

    def peer_p(d):
        return lax.rem(p + d, HEADS)

    def peer_chip(d):
        return lax.rem(chip + d, CHIPS)

    def back_chip(d):
        return lax.rem(chip + CHIPS - d, CHIPS)

    def remote(src, dst, ssem, rsem, dev):
        return pltpu.make_async_remote_copy(
            src_ref=src, dst_ref=dst, send_sem=ssem, recv_sem=rsem, device_id=dev, device_id_type=MESH
        )

    loads = [
        pltpu.make_async_copy(src, dst, in_sem.at[i])
        for i, (src, dst) in enumerate(
            (
                (pk, rows_in.at[0]), (pv, rows_in.at[1]), (pq, rows_in.at[2]), (pg, rows_in.at[3]),
                (ck.at[0], k_c), (cq.at[0], q_all.at[0:NC]), (cv.at[0], v_c), (cg.at[0], g_all.at[0:NC]),
                (lens, lens_in),
            )
        )
    ]
    for load in loads:
        load.start()

    barrier = pltpu.get_barrier_semaphore()
    for dc in range(CHIPS):
        for dp in range(HEADS):
            if dc or dp:
                pl.semaphore_signal(
                    barrier, inc=1, device_id=(peer_p(dp), peer_chip(dc) * 2 + core), device_id_type=MESH
                )
    pl.semaphore_signal(barrier, inc=1, device_id=(p, sibling), device_id_type=MESH)

    for load in loads[:4]:
        load.wait()
    for h in range(HEADS):
        cols = slice(h * HS, (h + 1) * HS)
        send_kv[h, 0] = rows_in[0, :, cols]
        send_kv[h, 1] = rows_in[1, :, cols]
        send_qg[h, 0] = rows_in[2, :, cols]
        send_qg[h, 1] = rows_in[3, :, cols]
    kv[0, 0, p] = send_kv[p]
    qg[p] = send_qg[p]

    pl.semaphore_wait(barrier, HEADS * CHIPS)

    for dc in range(CHIPS):
        for dp in range(HEADS):
            if dc or dp:
                remote(
                    send_kv.at[peer_p(dp)], kv.at[0, dc, p], s1.at[dc], r1.at[dc],
                    (peer_p(dp), peer_chip(dc) * 2 + core),
                ).start()
    for dp in range(1, HEADS):
        remote(send_qg.at[peer_p(dp)], qg.at[p], s2.at[0], r2.at[0], (peer_p(dp), g)).start()

    for load in loads[4:]:
        load.wait()
    length = lens_in[0, 0]

    def place(c, qn):
        return slice(c % 2 * CB, c % 2 * CB + CB), slice(c // 2 * qn, c // 2 * qn + qn)

    def scores(keys, values, q, gr, mask, e_ref, d_ref, rows, qs, qn):
        mx = jnp.full((8, qn), NEG, F)
        for c, r in enumerate(rows):
            k = keys(c)
            s = nt(jnp.concatenate([k, k], axis=1), q)
            keep = mask(c)
            if keep is not None:
                s = jnp.where(keep, s, NEG)
            sbuf[place(c, qn)] = s
            mx = jnp.maximum(mx, fold(s, jnp.max))
        m = rowmax(mx)
        l = jnp.zeros((8, qn), F)
        w = jnp.zeros((8, qn), F)
        for c, r in enumerate(rows):
            e = jnp.exp2(sbuf[place(c, qn)] - m)
            e_ref[r, qs] = e.astype(B)
            dp = nt(values(c), gr).astype(B)
            d_ref[r, qs] = dp
            l = l + fold(e, jnp.sum)
            w = w + fold(e * dp.astype(F), jnp.sum)
        return m, rowsum(l), rowsum(w)

    def grads(rows, qs, factor, delta, e_ref, d_ref):
        low = factor.astype(B)
        for r in rows:
            probs = e_ref[r, qs] * low
            e_ref[r, qs] = probs
            d_ref[r, qs] = probs * (d_ref[r, qs].astype(F) - delta).astype(B)

    diagonal = lax.broadcasted_iota(jnp.int32, (CB, CB), 0) <= lax.broadcasted_iota(jnp.int32, (CB, CB), 1)

    def split_scaled(rows):
        scaled = q_all[rows, :].astype(F) * SCALE2
        high = scaled.astype(B)
        q_two[rows, 0:HS] = high
        q_two[rows, HS:] = (scaled - high.astype(F)).astype(B)

    split_scaled(slice(0, NC))

    def cont_rows(i):
        return [slice(j * CB, (j + 1) * CB) for j in range(i + 1)]

    def cont_scores(i):
        rows = cont_rows(i)
        qs = rows[i]
        m, l, w = scores(
            lambda c: k_c[rows[c], :], lambda c: v_c[rows[c], :], q_two[qs, :], g_all[qs, :],
            lambda c: diagonal if c == i else None, e_c, d_c, rows, qs, CB,
        )
        stat[0, 0:1, qs] = m
        stat[0, 1:2, qs] = l
        stat[0, 2:3, qs] = w

    for i in range(NC // CB):
        cont_scores(i)

    forwards = []

    def forward(dc):
        at = kv.at[0, dc]
        whole = at if dc else kv.at[0, 0, 0 : HEADS - 1]
        remote(whole, whole, s1.at[dc], r1.at[dc], (p, sibling)).wait()
        c = remote(at, kv.at[1, dc], s3.at[dc], r3.at[dc], (p, sibling))
        c.start()
        forwards.append(c)

    def kv_rows(which, r):
        first = r.start // HS
        return kv[first // CHIPS, first % CHIPS : first % CHIPS + CB // HS, :, which].reshape(CB, HS)

    groups = {k + 1: (k * GK // 2, (k + 1) * GK // 2) for k in range(4)}
    own_rows = slice(NC, NQ)

    def group_rows(k):
        return [slice(r, r + CB) for r in range(groups[k][0], groups[k][1], CB)]

    def prompt_scores(k, qs, qn, mask):
        rows = group_rows(k)
        m, l, w = scores(
            lambda c: kv_rows(0, rows[c]), lambda c: kv_rows(1, rows[c]), q_two[qs, :], g_all[qs, :],
            lambda c: mask(rows[c]), e_p, d_p, rows, qs, qn,
        )
        stat[k, 0:1, qs] = m
        stat[k, 1:2, qs] = l
        stat[k, 2:3, qs] = w

    def member_scores(k):
        prompt_scores(k, slice(0, NC), NC, lambda r: None)

    def prompt_mask(r):
        row = lax.broadcasted_iota(jnp.int32, (CB, 1), 0)
        key_chip = chip + CHIPS - (r.start % GK // HS + row // HS)
        key_chip = jnp.where(key_chip >= CHIPS, key_chip - CHIPS, key_chip)
        key_group = key_chip * 2 + (other if r.start >= GK else core)
        key_pos = ((row % HS) // 16) * 256 + key_group * 16 + row % 16
        col = lax.broadcasted_iota(jnp.int32, (1, PQ), 1)
        query_pos = (col // 16) * 256 + g * 16 + col % 16
        return key_pos <= query_pos

    for dc in range(CHIPS // 2):
        forward(dc)
    member_scores(1)
    for dc in range(CHIPS // 2):
        forwards[dc].wait_recv()
    member_scores(3)
    for dc in range(CHIPS // 2, CHIPS):
        forward(dc)
    member_scores(2)
    seven = qg.at[0 : HEADS - 1]
    remote(seven, seven, s2.at[0], r2.at[0], (p, sibling)).wait()
    q_all[own_rows, :] = qg[:, 0].reshape(PQ, HS)
    g_all[own_rows, :] = qg[:, 1].reshape(PQ, HS)
    split_scaled(own_rows)
    for k in (1, 2, 3):
        prompt_scores(k, own_rows, PQ, prompt_mask)
    for dc in range(CHIPS // 2, CHIPS):
        forwards[dc].wait_recv()
    member_scores(4)
    prompt_scores(4, own_rows, PQ, prompt_mask)

    stat[0, 0:1, own_rows] = jnp.full((1, PQ), NEG, F)
    stat[0, 1:3, own_rows] = jnp.zeros((2, PQ), F)
    for i in range(NQ // PQ):
        qs = slice(i * PQ, (i + 1) * PQ)
        ms = [stat[k, 0:1, qs] for k in range(5)]
        top = ms[0]
        for m in ms[1:]:
            top = jnp.maximum(top, m)
        scale = [jnp.exp2(m - top) for m in ms]
        l = sum(scale[k] * stat[k, 1:2, qs] for k in range(5))
        w = sum(scale[k] * stat[k, 2:3, qs] for k in range(5))
        inv = 1.0 / l
        delta = w * inv
        if i < NC // PQ:
            live = (lax.broadcasted_iota(jnp.int32, (1, PQ), 1) + i * PQ) < length
            inv = jnp.where(live, inv, 0.0)
        for k in range(5):
            stat[k, 3:4, qs] = scale[k] * inv
        stat[0, 4:5, qs] = delta

    def prompt_grads(k):
        def body(i, carry):
            qs = pl.ds(pl.multiple_of(i * WB, WB), WB)
            grads(group_rows(k), qs, stat[k, 3:4, qs], stat[0, 4:5, qs], e_p, d_p)
            return carry

        lax.fori_loop(0, NC // WB, body, 0)
        grads(group_rows(k), own_rows, stat[k, 3:4, own_rows], stat[0, 4:5, own_rows], e_p, d_p)

    def parts(start, size):
        r = slice(start, start + size)
        return nn(d_p[r, :], q_all[...]) * SCALE, nn(e_p[r, :], g_all[...])

    halves = 2
    units = 4
    unit = GK // units
    prompt_grads(3)
    prompt_grads(4)
    to_sibling = []
    for u in range(halves):
        dk, dv = parts(GK + u * 2 * unit, 2 * unit)
        st_sib[u, 0] = dk.astype(B)
        st_sib[u, 1] = dv.astype(B)
        c = remote(st_sib.at[u], r_sib.at[u], s4.at[u], r4.at[u], (p, sibling))
        c.start()
        to_sibling.append(c)
    prompt_grads(1)
    prompt_grads(2)
    slot = p * CHIPS + chip
    per = CHIPS // units
    for u in range(units):
        dk, dv = parts(u * unit, unit)
        if u % 2 == 0:
            to_sibling[u // 2].wait_recv()
        at = slice(u * per, (u + 1) * per)
        share = slice(u % 2 * unit, u % 2 * unit + unit)
        st_own[at, :, 0] = (dk + r_sib[u // 2, 0, share].astype(F)).astype(B).reshape(per, HEADS, 16, HS)
        st_own[at, :, 1] = (dv + r_sib[u // 2, 1, share].astype(F)).astype(B).reshape(per, HEADS, 16, HS)
        for dc in range(u * per, (u + 1) * per):
            for dp in range(HEADS):
                if dc or dp:
                    remote(
                        st_own.at[dc, peer_p(dp)], r_own.at[slot], s5.at[0], r5.at[0],
                        (peer_p(dp), back_chip(dc) * 2 + core),
                    ).start()
    r_own[slot] = st_own[0, p]

    for start in range(0, NP, CB):
        r = slice(start, start + CB)
        kt_p[:, r] = kv_rows(0, r).T
    dq = nn(kt_p[...], d_p[:, own_rows]) * SCALE
    dq_out[...] = dq.T.astype(B).reshape(HEADS, 16, HS)
    for dp in range(1, HEADS):
        remote(dq_out.at[peer_p(dp)], dq_in.at[p], s6.at[0], r6.at[0], (peer_p(dp), g)).start()
    dq_in[p] = dq_out[p]

    kt_c[...] = k_c[...].T
    for i in range(NC // CB):
        qs = slice(i * CB, (i + 1) * CB)
        grads(cont_rows(i), qs, stat[0, 3:4, qs], stat[0, 4:5, qs], e_c, d_c)

    for i in range(NC // QB):
        qs = slice(i * QB, (i + 1) * QB)
        first = slice(i * QB, i * QB + CB)
        second = slice(i * QB + CB, (i + 1) * QB)
        dq = nn(kt_p[...], d_p[:, qs])
        if i:
            dq = dq + nn(kt_c[:, 0 : i * QB], d_c[0 : i * QB, qs])
        left = nn(kt_c[:, first], d_c[first, first])
        right = nn(kt_c[:, i * QB : (i + 1) * QB], d_c[i * QB : (i + 1) * QB, second])
        dq = (dq + jnp.concatenate([left, right], axis=1)) * SCALE
        o_dq[0, qs, :] = dq.astype(B).T

    for j in range(NC // CB):
        r = slice(j * CB, (j + 1) * CB)
        qs = slice(j * CB, NC)
        o_dk[0, r, :] = (nn(d_c[r, qs], q_all[qs, :]) * SCALE).astype(B)
        o_dv[0, r, :] = nn(e_c[r, qs], g_all[qs, :]).astype(B)

    seven = dq_in.at[0 : HEADS - 1]
    remote(seven, seven, s6.at[0], r6.at[0], (p, sibling)).wait()
    for h in range(HEADS):
        o_pdq[:, h * HS : (h + 1) * HS] = dq_in[h]

    arrived = r_own.at[0 : HEADS * CHIPS - 1]
    remote(arrived, arrived, s5.at[0], r5.at[0], (p, sibling)).wait()
    for h in range(HEADS):
        cols = slice(h * HS, (h + 1) * HS)
        total = jnp.sum(r_own[h * CHIPS : (h + 1) * CHIPS].astype(F), axis=0)
        o_pdk[:, cols] = total[0].astype(B)
        o_pdv[:, cols] = total[1].astype(B)

    for c in forwards:
        c.wait_send()
    for c in to_sibling:
        c.wait_send()


def hand_over(*refs):
    ins, outs, sem = refs[:6], refs[6:12], refs[12]
    copies = [pltpu.make_async_copy(a, b, sem.at[i]) for i, (a, b) in enumerate(zip(ins, outs))]
    for c in copies:
        c.start()
    for c in copies:
        c.wait()


def shards(prompt_q, prompt_k, prompt_v, prompt_grad, cont_q, cont_k, cont_v, cont_grad, lengths):
    vm = pl.BlockSpec(memory_space=pltpu.VMEM)
    hbm = pl.BlockSpec(memory_space=pltpu.HBM)
    dma = pltpu.SemaphoreType.DMA
    vmem = pltpu.VMEM
    shapes = [(16, HEADS * HS)] * 3 + [(1, NC, HS)] * 3
    results = pl.pallas_call(
        kernel,
        out_shape=[vmem(shape, B) for shape in shapes],
        in_specs=[hbm] * 9,
        out_specs=[vm] * 6,
        scratch_shapes=[
            vmem((NQ, HS), B),
            vmem((NC, HS), B),
            vmem((NC, HS), B),
            vmem((NQ, HS), B),
            vmem((4, 16, HEADS * HS), B),
            vmem((HS, NC), B),
            vmem((HS, NP), B),
            vmem((2, CHIPS, HEADS, 2, 16, HS), B),
            vmem((HEADS, 2, 16, HS), B),
            vmem((HEADS, 2, 16, HS), B),
            vmem((HEADS, 2, 16, HS), B),
            vmem((NQ, 2 * HS), B),
            vmem((2 * CB, NC), F),
            vmem((NP, NQ), B),
            vmem((NC, NC), B),
            vmem((NP, NQ), B),
            vmem((NC, NC), B),
            vmem((5, 8, NQ), F),
            vmem((2, 2, GK // 2, HS), B),
            vmem((2, 2, GK // 2, HS), B),
            vmem((CHIPS, HEADS, 2, 16, HS), B),
            vmem((HEADS * CHIPS, 2, 16, HS), B),
            vmem((HEADS, 16, HS), B),
            vmem((HEADS, 16, HS), B),
            pltpu.SMEM((1, 1), jnp.int32),
            dma((9,)),
            dma((CHIPS,)),
            dma((CHIPS,)),
            dma((1,)),
            dma((1,)),
            dma((CHIPS,)),
            dma((CHIPS,)),
            dma((2,)),
            dma((2,)),
        ]
        + [dma((1,))] * 4,
        compiler_params=pltpu.CompilerParams(
            collective_id=0, has_side_effects=True, vmem_limit_bytes=60 * 2**20
        ),
    )(prompt_q, prompt_k, prompt_v, prompt_grad, cont_q, cont_k, cont_v, cont_grad, lengths.reshape(1, 1))
    return pl.pallas_call(
        hand_over,
        out_shape=[jax.ShapeDtypeStruct(shape, B) for shape in shapes],
        in_specs=[vm] * 6,
        out_specs=[hbm] * 6,
        scratch_shapes=[dma((6,))],
    )(*[pltpu.with_memory_space_constraint(x, pltpu.VMEM) for x in results])


def solution(mesh):
    rows = P(("prompt", "group"), None)
    member = P("group", None, "prompt")
    return jax.shard_map(
        shards,
        mesh=mesh,
        in_specs=(rows,) * 4 + (member,) * 4 + (P("group"),),
        out_specs=(rows,) * 3 + (member,) * 3,
        check_vma=False,
    )
```
